32 devices in a mesh: ctx: 8 (over y, x, core), fsdp: 4 (over z).
Axes of the slice: x: 2, y: 2, z: 4, core: 2. Of those that a mesh axis runs over, the one named last changes fastest.
Arguments:
- hidden_in: bfloat16 [4, 4096, 768], P('fsdp', 'ctx'), may hold values from -6 to 6
- token_ids: int32 [4, 4096], P('fsdp', 'ctx'), may hold values from 0 to 50303, as said below
- hash_table: int32 [50304], replicated, may hold values from 0 to 31, as said below
- deal_order: int32 [8], replicated, may hold values from 0 to 7, each once
- qkv_weight: bfloat16 [768, 2304], P('fsdp'), may hold values from -0.21875 to 0.21875
- out_weight: bfloat16 [768, 768], P('fsdp'), may hold values from -6 to 6
- norm1_gain: bfloat16 [768], P('fsdp'), may hold values from 0.5 to 1.5
- norm1_bias: bfloat16 [768], P('fsdp'), may hold values from -1 to 1
- norm2_gain: bfloat16 [768], P('fsdp'), may hold values from 0.5 to 1.5
- norm2_bias: bfloat16 [768], P('fsdp'), may hold values from -1 to 1
- expert_in: bfloat16 [32, 768, 3072], P('ctx', None, 'fsdp'), may hold values from -0.21875 to 0.21875
- expert_out: bfloat16 [32, 768, 3072], P('ctx', None, 'fsdp'), may hold values from -0.109375 to 0.109375
- out_grad: bfloat16 [4, 4096, 768], P('fsdp', 'ctx'), may hold values from -6 to 6
Outputs:
- layer_out: bfloat16 [4, 4096, 768], P('fsdp', 'ctx')
- grad_hidden: float32 [4, 4096, 768], P('fsdp', 'ctx')
- grad_qkv: float32 [768, 2304], P('fsdp')
- grad_out_weight: float32 [768, 768], P('fsdp')
- grad_norm1_gain: float32 [768], P('fsdp')
- grad_norm1_bias: float32 [768], P('fsdp')
- grad_norm2_gain: float32 [768], P('fsdp')
- grad_norm2_bias: float32 [768], P('fsdp')
- grad_expert_in: float32 [32, 768, 3072], P('ctx', None, 'fsdp')
- grad_expert_out: float32 [32, 768, 3072], P('ctx', None, 'fsdp')
The draws below stay inside these ranges and needn't reach their ends.
Inputs may be any that keep to these rules, and one draw needn't show every extreme that they name: `token_ids`: in each aligned block of 512 rows of a sequence (the rows of one device), no expert e = hash_table[id] is named by more than 32 tokens, and some expert by exactly 32. `hash_table`: every expert is the value of exactly 1572 token ids.
All inputs are finite; a program needn't handle non-finite values.
Results may differ from the reference program's by a relative error of at most 0.02.
Values may be sent and summed in bfloat16 or wider, within the bound.
No kernel may reach another device: no remote copies, remote signals or barrier semaphores. Data moves between devices by JAX's collectives and lax.ppermute only.
A program may use at most 320 MiB of HBM per device.

```python
import jax
import jax.numpy as jnp
from jax import lax

D = 768
HEADS = 12
HD = 64
FF = 3072
VOCAB = 50304
BLK = 256
PAIRS = 1
EXPERTS = 32
TOK_DEV = 512
LEN = 4096
SEQS = 4
NB = 16
CAPE = 32
N_CTX = 8


def route_tables(key):
    base = jax.random.fold_in(key, 5813)
    shuffled = jax.random.permutation(jax.random.fold_in(base, 1), VOCAB).astype(jnp.int32)
    hash_rows = (shuffled % EXPERTS).astype(jnp.int32)
    inverse = jnp.argsort(shuffled).astype(jnp.int32)
    return (base, hash_rows, inverse)


def draw_hash_table(key, part):
    return route_tables(key)[1]


def draw_token_ids(key, part):
    base, hash_rows, inverse = route_tables(key)
    mean_load = TOK_DEV // EXPERTS
    slot_index = jnp.arange(TOK_DEV, dtype=jnp.int32)
    half_rows = TOK_DEV // 2
    quarter_rows = TOK_DEV // 4
    ranking = jnp.where(slot_index < half_rows, slot_index // (2 * mean_load), jnp.where(slot_index < half_rows + quarter_rows, EXPERTS // 4 + (slot_index - half_rows) // mean_load, EXPERTS // 2 + (slot_index - half_rows - quarter_rows) // (mean_load // 2)))

    def one_block(block_key):
        expert_order = jax.random.permutation(jax.random.fold_in(block_key, 1), EXPERTS).astype(jnp.int32)
        row_order = jax.random.permutation(jax.random.fold_in(block_key, 2), TOK_DEV).astype(jnp.int32)
        chosen = expert_order[ranking][row_order]
        pick_index = jax.random.randint(jax.random.fold_in(block_key, 3), (TOK_DEV,), 0, VOCAB // EXPERTS)
        return inverse[chosen + EXPERTS * pick_index]
    block_keys = jax.random.split(jax.random.fold_in(base, 2), SEQS * LEN // TOK_DEV)
    return jax.vmap(one_block)(block_keys).reshape(SEQS, LEN).astype(jnp.int32)


def block_levels(stream_key, extent, cuts, smallest, high):
    def one(position, shards_of):
        heights = jax.random.uniform(jax.random.fold_in(jax.random.fold_in(stream_key, 6), position), (shards_of,), jnp.float32, smallest / len(cuts), high / len(cuts))
        return jnp.repeat(jnp.exp(heights), extent[position] // shards_of).reshape((-1,) + (1,) * (len(extent) - position - 1))

    level = one(*cuts[0])
    for cut in cuts[1:]:
        level = level * one(*cut)
    return level


def noise(rng, extent, width, bound, cuts=(), held_as=jnp.bfloat16):
    array = jax.random.normal(rng, extent, jnp.float32) * width
    if len(cuts) > 0:
        array = block_levels(rng, extent, cuts, -0.22, 0.18) * array
    return jnp.clip(array, min=-bound, max=bound).astype(held_as)


def setup_inputs(seed: int = 0) -> dict:
    seeds = jax.random.split(jax.random.key(seed), 14)
    hidden_in = noise(seeds[0], (SEQS, LEN, D), 1.0, 6.0, ((0, 4), (1, 8)))
    token_ids = draw_token_ids(jax.random.fold_in(seeds[13], 71), 0)
    hash_table = draw_hash_table(jax.random.fold_in(seeds[13], 71), 0)
    deal_order = jax.random.permutation(seeds[3], N_CTX * PAIRS).astype(jnp.int32)
    qkv_weight = noise(seeds[4], (D, 3 * D), D ** -0.5, 0.21875, ((0, 4),))
    out_weight = noise(seeds[5], (D, D), ((LEN // 4) ** 0.5 * D ** -0.5), 6.0, ((0, 4),))
    norm1_gain = jnp.clip(1.0 + 0.1 * jax.random.normal(seeds[6], (D,), jnp.float32), 0.5, 1.5).astype(jnp.bfloat16)
    norm1_bias = noise(seeds[7], (D,), 0.2, 1.0, ((0, 4),))
    norm2_gain = jnp.clip(1.0 + 0.1 * jax.random.normal(seeds[8], (D,), jnp.float32), 0.5, 1.5).astype(jnp.bfloat16)
    norm2_bias = noise(seeds[9], (D,), 0.2, 1.0, ((0, 4),))
    expert_in = noise(seeds[10], (EXPERTS, D, FF), D ** -0.5, 0.21875, ((0, 8), (2, 4)))
    expert_out = noise(seeds[11], (EXPERTS, D, FF), FF ** -0.5, 0.109375, ((0, 8), (2, 4)))
    out_grad = noise(seeds[12], (SEQS, LEN, D), 1.0, 6.0, ((0, 4), (1, 8)))
    return dict(hidden_in=hidden_in, token_ids=token_ids, hash_table=hash_table, deal_order=deal_order, qkv_weight=qkv_weight, out_weight=out_weight, norm1_gain=norm1_gain, norm1_bias=norm1_bias, norm2_gain=norm2_gain, norm2_bias=norm2_bias, expert_in=expert_in, expert_out=expert_out, out_grad=out_grad)


@jax.custom_vjp
def low(v):
    return lax.optimization_barrier(v.astype(jnp.bfloat16)).astype(jnp.float32)

@jax.custom_vjp
def low_back(v):
    return v

def low_keep(v):
    return (low(v), None)

def low_pass(kept, grad):
    return (grad,)

def back_keep(v):
    return (v, None)

def back_low(kept, grad):
    return (low(grad),)
low.defvjp(low_keep, low_pass)
low_back.defvjp(back_keep, back_low)
epsilon = 1e-05
masked_value = -1e+30
highest = lax.Precision.HIGHEST

def layer_norm(values, norm_gain, norm_bias):
    center = lax.optimization_barrier(jnp.mean(values, axis=-1, keepdims=True))
    offset = values - center
    spread = lax.optimization_barrier(jnp.mean(offset * offset, axis=-1, keepdims=True))
    return offset * lax.rsqrt(spread + epsilon) * norm_gain + norm_bias

def block_numbers(deal_order):
    pair_table = deal_order.reshape(N_CTX, PAIRS)
    block_table = jnp.concatenate([pair_table, NB - 1 - pair_table], axis=1)
    return jnp.repeat(block_table.reshape(-1), BLK).astype(jnp.int32)

def attend_rows(query_block, query_ids, key_heads, value_heads, key_ids):
    scores = jnp.einsum('qhd,khd->hqk', query_block, key_heads, precision=highest) * HD ** (-0.5)
    scores = low_back(scores)
    allowed = key_ids[None, None, :] <= query_ids[None, :, None]
    scores = jnp.where(allowed, scores, masked_value)
    largest = lax.optimization_barrier(jnp.max(scores, axis=-1, keepdims=True))
    weights = jnp.where(allowed, jnp.exp(scores - largest), 0.0)
    weights = low(weights / lax.optimization_barrier(jnp.sum(weights, axis=-1, keepdims=True)))
    return jnp.einsum('hqk,khd->qhd', weights, value_heads, precision=highest)

def attention_sequence(normed, qkv_weight, block_ids):
    projected = low_back(low(jnp.dot(normed, qkv_weight, precision=highest)))
    query_heads = projected[:, :D].reshape(LEN, HEADS, HD)
    key_heads = projected[:, D:2 * D].reshape(LEN, HEADS, HD)
    value_heads = projected[:, 2 * D:].reshape(LEN, HEADS, HD)
    step_rows = 512 if LEN % 512 == 0 else LEN
    query_blocks = query_heads.reshape(LEN // step_rows, step_rows, HEADS, HD)
    id_blocks = block_ids.reshape(LEN // step_rows, step_rows)
    checked = jax.checkpoint(attend_rows)

    def one_block(block_item):
        return checked(block_item[0], block_item[1], key_heads, value_heads, block_ids)
    return lax.map(one_block, (query_blocks, id_blocks)).reshape(LEN, D)

def forward(hidden, qkv_weight, out_weight, norm1_gain, norm1_bias, norm2_gain, norm2_bias, expert_in, expert_out, expert_of, block_ids):

    def per_sequence(rows_in):
        normed = low(layer_norm(rows_in, norm1_gain, norm1_bias))
        attended = low_back(low(attention_sequence(normed, qkv_weight, block_ids)))
        middle = rows_in + low_back(jnp.dot(attended, out_weight, precision=highest))
        return (middle, low_back(low(layer_norm(middle, norm2_gain, norm2_bias))))
    middle, normed_two = lax.map(per_sequence, hidden)
    flat_rows = normed_two.reshape(SEQS * LEN, D)
    most_rows = CAPE * SEQS * N_CTX

    def one_expert(expert_item):
        first_weight, second_weight, number = expert_item
        member = expert_of == number
        picked = jnp.nonzero(member, size=most_rows, fill_value=0)[0].astype(jnp.int32)
        live_rows = (jnp.arange(most_rows, dtype=jnp.int32) < jnp.sum(member.astype(jnp.int32))).astype(jnp.float32)
        pre_act = low_back(jnp.dot(flat_rows[picked], first_weight, precision=highest))
        activated = low(jax.nn.gelu(pre_act, approximate=True))
        result = low_back(low(jnp.dot(activated, second_weight.T, precision=highest)))
        return (result * live_rows[:, None], picked)
    results, picked_rows = lax.map(jax.checkpoint(one_expert), (expert_in, expert_out, jnp.arange(EXPERTS, dtype=jnp.int32)))
    expert_total = jnp.zeros((SEQS * LEN, D), jnp.float32).at[picked_rows.reshape(-1)].add(results.reshape(-1, D))
    return middle + expert_total.reshape(SEQS, LEN, D)

def reference(hidden_in, token_ids, hash_table, deal_order, qkv_weight, out_weight, norm1_gain, norm1_bias, norm2_gain, norm2_bias, expert_in, expert_out, out_grad):
    expert_of = hash_table[token_ids.reshape(-1)].astype(jnp.int32)
    block_ids = block_numbers(deal_order)
    float_args = tuple((array_in.astype(jnp.float32) for array_in in (hidden_in, qkv_weight, out_weight, norm1_gain, norm1_bias, norm2_gain, norm2_bias, expert_in, expert_out)))

    def wrapped_forward(*params_in):
        return forward(*params_in, expert_of, block_ids)
    layer_out, pullback = jax.vjp(wrapped_forward, *float_args)
    gradients = pullback(out_grad.astype(jnp.float32))
    return (layer_out.astype(jnp.bfloat16), gradients[0], gradients[1], gradients[2], gradients[3], gradients[4], gradients[5], gradients[6], gradients[7], gradients[8])
```

```python
from functools import partial

import jax
import jax.numpy as jnp
from jax import lax
from jax.experimental import pallas as pl
from jax.experimental.pallas import tpu as pltpu
from jax.sharding import PartitionSpec as P
from math import gcd

HEADS = 12
HD = 64
BLK = 256
TOK_DEV = 512
epsilon = 1e-05
masked_value = -1e30
bf16 = jnp.bfloat16
f32 = jnp.float32
NT = (((1,), (1,)), ((), ()))
NN = (((1,), (0,)), ((), ()))
TN = (((0,), (0,)), ((), ()))
VMEM_LIMIT = 56 * 1024 * 1024


def dot(a, b, dims=NN):
    return lax.dot_general(a, b, dims, preferred_element_type=f32)


def swap(value, axis, offset):
    size = lax.axis_size(axis)
    return lax.ppermute(value, axis, [(i, i ^ offset) for i in range(size)])


def in_order(pieces, index):
    count, bit = len(pieces), 1
    while bit < count:
        odd = (index & bit) != 0
        pieces = [jnp.where(odd, pieces[i ^ bit], pieces[i]) for i in range(count)]
        bit *= 2
    return pieces


def norm_stats(values):
    center = jnp.mean(values, axis=-1, keepdims=True)
    offset = values - center
    scale = lax.rsqrt(jnp.mean(offset * offset, axis=-1, keepdims=True) + epsilon)
    return offset * scale, scale


def norm_back(normal, scale, gain, grad):
    inner = grad * gain
    return scale * (
        inner
        - jnp.mean(inner, axis=-1, keepdims=True)
        - normal * jnp.mean(inner * normal, axis=-1, keepdims=True)
    )


def masked_heads(rows, heads):
    lane = lax.broadcasted_iota(jnp.int32, rows.shape, 1) // HD
    return [jnp.where(lane == h, rows, jnp.zeros_like(rows)) for h in range(heads)]


def chunk_places(block, step, place_ref):
    first = step * 2
    second = jnp.minimum(first + 1, block)
    bias = jnp.where(first + 1 <= block, 0.0, masked_value).astype(f32)
    return (
        pl.multiple_of(place_ref[first] * BLK, BLK),
        pl.multiple_of(place_ref[second] * BLK, BLK),
        bias,
    )


def attend_kernel(heads, block_ref, place_ref, q_ref, k_ref, vt_ref, att_ref, att_t_ref, lse_ref, acc_ref):
    block = block_ref[pl.program_id(0)]
    queries = masked_heads(q_ref[...], heads)
    acc_ref[...] = jnp.zeros_like(acc_ref)

    def step(index, state):
        top, total = state
        one, two, bias = chunk_places(block, index, place_ref)
        keys = jnp.concatenate([k_ref[pl.ds(one, BLK), :], k_ref[pl.ds(two, BLK), :]], axis=0)
        values = jnp.concatenate([vt_ref[:, pl.ds(one, BLK)], vt_ref[:, pl.ds(two, BLK)]], axis=1)
        tops, totals = [], []
        for h in range(heads):
            scores = dot(keys, queries[h], NT)
            low, high = scores[:BLK], scores[BLK:] + bias
            new_top = jnp.maximum(
                top[h], jnp.max(jnp.maximum(low, high), axis=0, keepdims=True)
            )
            factor = jnp.exp(top[h] - new_top)
            low, high = jnp.exp(low - new_top), jnp.exp(high - new_top)
            tops.append(new_top)
            totals.append(total[h] * factor + jnp.sum(low + high, axis=0, keepdims=True))
            weights = jnp.concatenate([low.astype(bf16), high.astype(bf16)], axis=0)
            rows = slice(h * HD, (h + 1) * HD)
            acc_ref[rows, :] = acc_ref[rows, :] * factor + dot(values[rows, :], weights)
        return tuple(tops), tuple(totals)

    start = (
        tuple(jnp.full((1, BLK), masked_value, f32) for _ in range(heads)),
        tuple(jnp.zeros((1, BLK), f32) for _ in range(heads)),
    )
    top, total = lax.fori_loop(0, (block + 2) // 2, step, start)
    for h in range(heads):
        rows = slice(h * HD, (h + 1) * HD)
        acc_ref[rows, :] = acc_ref[rows, :] / total[h]
        lse_ref[0, h : h + 1, :] = top[h] + jnp.log(total[h])
    att_t_ref[...] = acc_ref[...]
    att_ref[...] = jnp.transpose(acc_ref[...]).astype(bf16)


def attend(block_of, place_of, queries, keys, values_t):
    rows, width = queries.shape
    heads = width // HD
    blocks = rows // BLK
    whole = lambda shape: pl.BlockSpec(shape, lambda i, *_: (0, 0), pipeline_mode=pl.Buffered(1))
    return pl.pallas_call(
        partial(attend_kernel, heads),
        grid_spec=pltpu.PrefetchScalarGridSpec(
            num_scalar_prefetch=2,
            grid=(blocks,),
            in_specs=[
                pl.BlockSpec((BLK, width), lambda i, *_: (i, 0)),
                whole(keys.shape),
                whole(values_t.shape),
            ],
            out_specs=[
                pl.BlockSpec((BLK, width), lambda i, *_: (i, 0)),
                pl.BlockSpec((width, BLK), lambda i, *_: (0, i)),
                pl.BlockSpec((1, heads, BLK), lambda i, *_: (i, 0, 0)),
            ],
            scratch_shapes=[pltpu.VMEM((width, BLK), f32)],
        ),
        out_shape=[
            jax.ShapeDtypeStruct((rows, width), bf16),
            jax.ShapeDtypeStruct((width, rows), f32),
            jax.ShapeDtypeStruct((blocks, heads, BLK), f32),
        ],
        compiler_params=pltpu.CompilerParams(vmem_limit_bytes=VMEM_LIMIT),
        cost_estimate=pl.CostEstimate(
            flops=16 * rows * keys.shape[0] * width,
            bytes_accessed=8 * keys.shape[0] * width,
            transcendentals=rows * keys.shape[0] * heads // 2,
        ),
        name="attend",
    )(block_of, place_of, queries, keys, values_t)


def attend_back_kernel(
    heads, block_ref, place_ref, q_ref, g_ref, att_t_ref, lse_ref, k_ref, v_ref, kt_ref,
    gq_ref, gk_ref, gv_ref, gqt_ref, gk_acc, gv_acc,
):
    turn = pl.program_id(0)
    block = block_ref[turn]

    @pl.when(turn == 0)
    def _():
        gk_acc[...] = jnp.zeros_like(gk_acc)
        gv_acc[...] = jnp.zeros_like(gv_acc)

    queries = masked_heads(q_ref[...], heads)
    grads = masked_heads(g_ref[...], heads)
    prod = jnp.transpose(g_ref[...].astype(f32)) * att_t_ref[...]
    deltas = [jnp.sum(prod[h * HD : (h + 1) * HD], axis=0, keepdims=True) for h in range(heads)]
    logs = [lse_ref[0, h : h + 1, :] for h in range(heads)]
    gqt_ref[...] = jnp.zeros_like(gqt_ref)

    def step(index, carry):
        one, two, bias = chunk_places(block, index, place_ref)
        keys = jnp.concatenate([k_ref[pl.ds(one, BLK), :], k_ref[pl.ds(two, BLK), :]], axis=0)
        values = jnp.concatenate([v_ref[pl.ds(one, BLK), :], v_ref[pl.ds(two, BLK), :]], axis=0)
        keys_t = jnp.concatenate([kt_ref[:, pl.ds(one, BLK)], kt_ref[:, pl.ds(two, BLK)]], axis=1)
        gk, gv = None, None
        for h in range(heads):
            scores = dot(keys, queries[h], NT)
            low = jnp.exp(scores[:BLK] - logs[h])
            high = jnp.exp(scores[BLK:] + (bias - logs[h]))
            probs = jnp.concatenate([low, high], axis=0)
            grad_scores = (probs * (dot(values, grads[h], NT) - deltas[h])).astype(bf16)
            rows = slice(h * HD, (h + 1) * HD)
            gqt_ref[rows, :] += dot(keys_t[rows, :], grad_scores)
            gv_h = dot(probs.astype(bf16), grads[h])
            gk_h = dot(grad_scores, queries[h])
            gk, gv = (gk_h, gv_h) if h == 0 else (gk + gk_h, gv + gv_h)
        gk_acc[pl.ds(one, BLK), :] += gk[:BLK]
        gv_acc[pl.ds(one, BLK), :] += gv[:BLK]
        gk_acc[pl.ds(two, BLK), :] += gk[BLK:]
        gv_acc[pl.ds(two, BLK), :] += gv[BLK:]
        return carry

    lax.fori_loop(0, (block + 2) // 2, step, 0)
    gq_ref[...] = (jnp.transpose(gqt_ref[...]) * HD ** (-0.5)).astype(bf16)

    @pl.when(turn == pl.num_programs(0) - 1)
    def _():
        gk_ref[...] = gk_acc[...].astype(bf16)
        gv_ref[...] = gv_acc[...].astype(bf16)


def attend_back(block_of, place_of, queries, grads, att_t, logs, keys, values, keys_t):
    rows, width = queries.shape
    heads = width // HD
    blocks = rows // BLK
    whole = lambda shape: pl.BlockSpec(shape, lambda i, *_: (0, 0), pipeline_mode=pl.Buffered(1))
    row_spec = pl.BlockSpec((BLK, width), lambda i, *_: (i, 0))
    return pl.pallas_call(
        partial(attend_back_kernel, heads),
        grid_spec=pltpu.PrefetchScalarGridSpec(
            num_scalar_prefetch=2,
            grid=(blocks,),
            in_specs=[
                row_spec,
                row_spec,
                pl.BlockSpec((width, BLK), lambda i, *_: (0, i)),
                pl.BlockSpec((1, heads, BLK), lambda i, *_: (i, 0, 0)),
                whole(keys.shape),
                whole(values.shape),
                whole(keys_t.shape),
            ],
            out_specs=[row_spec, whole(keys.shape), whole(values.shape)],
            scratch_shapes=[
                pltpu.VMEM((width, BLK), f32),
                pltpu.VMEM(keys.shape, f32),
                pltpu.VMEM(values.shape, f32),
            ],
        ),
        out_shape=[
            jax.ShapeDtypeStruct((rows, width), bf16),
            jax.ShapeDtypeStruct(keys.shape, bf16),
            jax.ShapeDtypeStruct(values.shape, bf16),
        ],
        compiler_params=pltpu.CompilerParams(vmem_limit_bytes=VMEM_LIMIT),
        cost_estimate=pl.CostEstimate(
            flops=40 * rows * keys.shape[0] * width,
            bytes_accessed=16 * keys.shape[0] * width,
            transcendentals=rows * keys.shape[0] * heads // 2,
        ),
        name="attend_back",
    )(block_of, place_of, queries, grads, att_t, logs, keys, values, keys_t)


def expert_kernel(x_ref, gy_ref, first_ref, second_ref, act_ref, gpre_ref, gn_ref, ey_ref):
    flat = lambda ref: ref[...].reshape(-1, ref.shape[-1])
    first, second = first_ref[0], second_ref[0]
    pre = dot(flat(x_ref), first)
    inner = 0.7978845608028654 * (pre + 0.044715 * (pre * pre * pre))
    bend = jnp.tanh(inner)
    half = 0.5 * (1.0 + bend)
    act = (pre * half).astype(bf16)
    slope = half + 0.5 * pre * (1.0 - bend * bend) * (
        0.7978845608028654 * (1.0 + 3 * 0.044715 * (pre * pre))
    )
    gpre = (dot(flat(gy_ref), second) * slope).astype(bf16)
    act_ref[...] = act.reshape(act_ref.shape)
    gpre_ref[...] = gpre.reshape(gpre_ref.shape)
    gn_ref[...] = dot(gpre, first, NT).astype(bf16).reshape(gn_ref.shape)
    ey_ref[...] = dot(act, second, NT).astype(bf16).reshape(ey_ref.shape)


def expert_step(tokens, grads, first, second):
    sources, experts, room, width = tokens.shape
    hidden = first.shape[2]
    token_spec = pl.BlockSpec((sources, 1, room, width), lambda e: (0, e, 0, 0))
    hidden_spec = pl.BlockSpec((sources, 1, room, hidden), lambda e: (0, e, 0, 0))
    weight_spec = pl.BlockSpec((1, width, hidden), lambda e: (e, 0, 0))
    like = lambda last: jax.ShapeDtypeStruct((sources, experts, room, last), bf16)
    return pl.pallas_call(
        expert_kernel,
        grid=(experts,),
        in_specs=[token_spec, token_spec, weight_spec, weight_spec],
        out_specs=[hidden_spec, hidden_spec, token_spec, token_spec],
        out_shape=[like(hidden), like(hidden), like(width), like(width)],
        compiler_params=pltpu.CompilerParams(vmem_limit_bytes=VMEM_LIMIT),
        cost_estimate=pl.CostEstimate(
            flops=8 * sources * experts * room * width * hidden,
            bytes_accessed=4 * first.size + 12 * tokens.size,
            transcendentals=sources * experts * room * hidden,
        ),
        name="expert_step",
    )(tokens, grads, first, second)


def expert_grad_kernel(parts, *refs):
    flat = lambda ref: ref[...].reshape(-1, ref.shape[-1])
    stack = lambda some: jnp.concatenate([flat(r) for r in some], axis=0)
    ins, (gfirst_ref, gsecond_ref) = refs[: 4 * parts], refs[4 * parts :]
    tokens, grads, acts, gpres = (stack(ins[i * parts : (i + 1) * parts]) for i in range(4))
    gfirst_ref[0] = dot(tokens, gpres, TN)
    gsecond_ref[0] = dot(grads, acts, TN)


def expert_grads(tokens, grads, acts, gpres):
    parts = len(tokens)
    sources, experts, room, width = tokens[0].shape
    hidden = acts[0].shape[3]
    spec = lambda last: pl.BlockSpec((sources, 1, room, last), lambda e: (0, e, 0, 0))
    out_spec = pl.BlockSpec((1, width, hidden), lambda e: (e, 0, 0))
    out = jax.ShapeDtypeStruct((experts, width, hidden), f32)
    return pl.pallas_call(
        partial(expert_grad_kernel, parts),
        grid=(experts,),
        in_specs=[spec(width)] * (2 * parts) + [spec(hidden)] * (2 * parts),
        out_specs=[out_spec, out_spec],
        out_shape=[out, out],
        compiler_params=pltpu.CompilerParams(vmem_limit_bytes=VMEM_LIMIT),
        cost_estimate=pl.CostEstimate(
            flops=4 * parts * sources * experts * room * width * hidden,
            bytes_accessed=8 * experts * width * hidden,
            transcendentals=0,
        ),
        name="expert_grads",
    )(*tokens, *grads, *acts, *gpres)


def reduce_stage(parts, index, axis, stride):
    count = parts.shape[0]
    pick = lambda k: lax.dynamic_index_in_dim(parts, index ^ k, 0, keepdims=False)
    total = pick(0)
    for k in range(1, count):
        total = total + swap(pick(k).astype(bf16), axis, k * stride).astype(f32)
    return total


def gather_stage(part, count, index, axis, stride):
    pieces = [part] + [swap(part, axis, k * stride) for k in range(1, count)]
    return in_order(pieces, index)


def local(
    hidden_in, token_ids, hash_table, deal_order, qkv_weight, out_weight,
    norm1_gain, norm1_bias, norm2_gain, norm2_bias, expert_in, expert_out, out_grad,
):
    devices = lax.axis_size("ctx")
    position = lax.axis_index("ctx")
    planes = lax.axis_size("fsdp")
    plane = lax.axis_index("fsdp")
    width = hidden_in.shape[2]
    local_experts = expert_in.shape[0]
    experts = local_experts * devices
    room = 2 * TOK_DEV // experts
    groups = gcd(HEADS, devices)
    cores = devices // groups
    group, core = position // cores, position % cores
    span = width // groups

    own_hidden = hidden_in[0]
    out_cot = out_grad[0]

    hidden = jnp.concatenate(
        [own_hidden] + [swap(own_hidden, "ctx", j * cores) for j in range(1, groups)]
    ).astype(f32)

    cut = lambda part: lax.dynamic_slice_in_dim(qkv_weight, part * width + group * span, span, 1)
    own_cols = jnp.concatenate([cut(0), cut(1), cut(2)], axis=1)
    own_vecs = jnp.stack([norm1_gain, norm1_bias, norm2_gain, norm2_bias])
    cols = jnp.concatenate(gather_stage(own_cols, planes, plane, "fsdp", 1))
    vecs = jnp.concatenate(gather_stage(own_vecs, planes, plane, "fsdp", 1), axis=1).astype(f32)
    out_full = jnp.concatenate(gather_stage(out_weight, planes, plane, "fsdp", 1))
    gain_one, bias_one, gain_two, bias_two = (vecs[i] for i in range(4))
    wq, wk, wv = cols[:, :span], cols[:, span : 2 * span], cols[:, 2 * span :]

    expert_of = hash_table[token_ids[0]]
    same = expert_of[:, None] == expert_of[None, :]
    before = lax.broadcasted_iota(jnp.int32, same.shape, 1) < lax.broadcasted_iota(jnp.int32, same.shape, 0)
    rank = jnp.sum((same & before).astype(jnp.int32), axis=1)
    slot = ((expert_of // local_experts) ^ position) * (local_experts * room) + (
        expert_of % local_experts
    ) * room + rank
    slots = [slot, None] + [swap(slot, "fsdp", k) for k in range(2, planes)]
    all_slots = experts * room
    one_hot = lambda s: (
        lax.broadcasted_iota(jnp.int32, (all_slots, TOK_DEV), 0) == s[None, :]
    ).astype(bf16)
    places = [None if s is None else one_hot(s) for s in slots]

    def exchange(rows):
        pieces = rows.reshape(devices, local_experts * room, width)
        got = [pieces[0]] + [swap(pieces[k], "ctx", k) for k in range(1, devices)]
        return jnp.stack(got)

    def dispatch(rows):
        far = [None, None] + [swap(rows, "fsdp", k) for k in range(2, planes)]
        first = exchange(dot(places[0], rows).astype(bf16))
        got = [first, swap(first, "fsdp", 1)]
        for k in range(2, planes):
            got.append(exchange(dot(places[k], far[k]).astype(bf16)))
        return [g.reshape(devices, local_experts, room, width) for g in got]

    def combine(parts):
        parts = [p.reshape(devices, local_experts * room, width) for p in parts]
        total = None
        for k in range(planes - 1, 1, -1):
            back = dot(places[k], exchange(parts[k]).reshape(all_slots, width), TN).astype(bf16)
            back = swap(back, "fsdp", k).astype(f32)
            total = back if total is None else total + back
        near = (parts[0].astype(f32) + swap(parts[1], "fsdp", 1).astype(f32)).astype(bf16)
        near = dot(places[0], exchange(near).reshape(all_slots, width), TN)
        return near if total is None else near + total

    grads_sent = dispatch(out_cot)

    normal_one, scale_one = norm_stats(hidden)
    normed_one = (normal_one * gain_one + bias_one).astype(bf16)
    queries = (dot(normed_one, wq).astype(bf16) * HD ** (-0.5)).astype(bf16)
    own_keys = dot(normed_one, wk).astype(bf16)
    own_values = dot(normed_one, wv).astype(bf16)
    keys = jnp.concatenate([own_keys] + [swap(own_keys, "ctx", k) for k in range(1, cores)])
    values = jnp.concatenate([own_values] + [swap(own_values, "ctx", k) for k in range(1, cores)])
    keys_t, values_t = keys.T, values.T
    low_of = lambda g, s: deal_order[(group ^ g) * cores + (core ^ s)]
    numbers = []
    for s in range(cores):
        for g in range(groups):
            low = low_of(g, s)
            numbers += [low, 2 * devices - 1 - low]
    numbers = jnp.stack(numbers)
    count = 2 * devices
    place_of = jnp.sum(
        jnp.where(
            numbers[None, :] == jnp.arange(count, dtype=jnp.int32)[:, None],
            jnp.arange(count, dtype=jnp.int32)[None, :],
            0,
        ),
        axis=1,
    ).astype(jnp.int32)
    block_of = numbers[: 2 * groups]
    att, att_t, logs = attend(block_of, place_of, queries, keys, values_t)
    atts = [att[:TOK_DEV]] + [
        swap(att[j * TOK_DEV : (j + 1) * TOK_DEV], "ctx", j * cores) for j in range(1, groups)
    ]
    out_rows = [
        lax.dynamic_slice_in_dim(out_full, (group ^ j) * span, span, 0) for j in range(groups)
    ]
    own_float = own_hidden.astype(f32)
    middle = own_float + sum(dot(a, w) for a, w in zip(atts, out_rows))
    normal_two, scale_two = norm_stats(middle)
    normed_two = (normal_two * gain_two + bias_two).astype(bf16)

    tokens_sent = dispatch(normed_two)
    acts, gpres, gnorms, eys = [], [], [], []
    for k in range(planes):
        act, gpre, gn, ey = expert_step(tokens_sent[k], grads_sent[k], expert_in, expert_out)
        acts.append(act)
        gpres.append(gpre)
        gnorms.append(gn)
        eys.append(ey)
    grad_normed_two = combine(gnorms)
    grad_expert_in, grad_expert_out = expert_grads(tokens_sent, grads_sent, acts, gpres)
    token_y = combine(eys)
    layer_out = (middle + token_y).astype(bf16)

    grad_normed_two = grad_normed_two.astype(bf16).astype(f32)
    grad_gain_two = jnp.sum(grad_normed_two * normal_two, axis=0)
    grad_bias_two = jnp.sum(grad_normed_two, axis=0)
    grad_middle = out_cot.astype(f32) + norm_back(normal_two, scale_two, gain_two, grad_normed_two)
    grad_branch = grad_middle.astype(bf16)
    gatts = [dot(grad_branch, w, NT).astype(bf16) for w in out_rows]
    gatt = jnp.concatenate([gatts[0]] + [swap(gatts[j], "ctx", j * cores) for j in range(1, groups)])
    grad_out_rows = in_order([dot(a, grad_branch, TN) for a in atts], group)
    pad = lambda some: jnp.stack(some + [jnp.zeros_like(some[0])] * (128 - len(some)), axis=1)
    outs = jnp.concatenate(
        [jnp.concatenate(grad_out_rows), pad([grad_gain_two, grad_bias_two])], axis=1
    )

    grad_q, grad_k, grad_v = attend_back(
        block_of, place_of, queries, gatt, att_t, logs, keys, values, keys_t
    )
    half = groups * TOK_DEV

    def meet(some):
        total = some[:half].astype(f32)
        for k in range(1, cores):
            total = total + swap(some[k * half : (k + 1) * half], "ctx", k).astype(f32)
        return total.astype(bf16)

    grad_cols = jnp.concatenate([grad_q, meet(grad_k), meet(grad_v)], axis=1)
    grad_rows = dot(grad_cols, cols, NT)
    pieces = [grad_rows[j * TOK_DEV : (j + 1) * TOK_DEV] for j in range(groups)]
    grad_normed_one = pieces[0] + sum(
        swap(pieces[j].astype(bf16), "ctx", j * cores).astype(f32) for j in range(1, groups)
    )
    grad_hidden = grad_middle + norm_back(
        normal_one[:TOK_DEV], scale_one[:TOK_DEV], gain_one, grad_normed_one
    )
    grad_weights = dot(normed_one, grad_cols, TN)
    grad_gain_one = jnp.sum(grad_rows * normal_one, axis=0)
    grad_bias_one = jnp.sum(grad_rows, axis=0)
    mixed = jnp.concatenate([grad_weights, pad([grad_gain_one, grad_bias_one])], axis=1)

    rows = width // planes
    wide = mixed.shape[1]
    part = reduce_stage(
        jnp.moveaxis(mixed.reshape(planes, cores, rows // cores, wide), 1, 0), core, "ctx", 1
    )
    part = reduce_stage(part, plane, "fsdp", 1).astype(bf16)
    part = jnp.stack(gather_stage(part, groups, group, "ctx", cores))
    part = jnp.concatenate(gather_stage(part, cores, core, "ctx", 1), axis=1).astype(f32)
    grad_qkv = jnp.transpose(
        part[:, :, : 3 * span].reshape(groups, rows, 3, span), (1, 2, 0, 3)
    ).reshape(rows, 3 * width)
    vec_one = jnp.sum(part[:, :, 3 * span : 3 * span + 2], axis=0)

    wide = outs.shape[1]
    part = reduce_stage(
        jnp.moveaxis(outs.reshape(planes, cores, rows // cores, wide), 1, 0), core, "ctx", 1
    )
    part = reduce_stage(
        jnp.moveaxis(part.reshape(planes, groups, rows // devices, wide), 1, 0), group, "ctx", cores
    )
    part = reduce_stage(part, plane, "fsdp", 1).astype(bf16)
    part = jnp.concatenate(gather_stage(part, groups, group, "ctx", cores))
    part = jnp.concatenate(gather_stage(part, cores, core, "ctx", 1)).astype(f32)
    grad_out_weight = part[:, :width]
    vec_two = part[:, width : width + 2]
    return (
        layer_out[None],
        grad_hidden[None],
        grad_qkv,
        grad_out_weight,
        vec_one[:, 0],
        vec_one[:, 1],
        vec_two[:, 0],
        vec_two[:, 1],
        grad_expert_in,
        grad_expert_out,
    )


def solution(mesh):
    return jax.shard_map(
        local,
        mesh=mesh,
        in_specs=(
            P("fsdp", "ctx", None),
            P("fsdp", "ctx"),
            P(),
            P(),
            P("fsdp", None),
            P("fsdp", None),
            P("fsdp"),
            P("fsdp"),
            P("fsdp"),
            P("fsdp"),
            P("ctx", None, "fsdp"),
            P("ctx", None, "fsdp"),
            P("fsdp", "ctx", None),
        ),
        out_specs=(
            P("fsdp", "ctx", None),
            P("fsdp", "ctx", None),
            P("fsdp", None),
            P("fsdp", None),
            P("fsdp"),
            P("fsdp"),
            P("fsdp"),
            P("fsdp"),
            P("ctx", None, "fsdp"),
            P("ctx", None, "fsdp"),
        ),
        check_vma=False,
    )
```

```python
from functools import partial
from math import gcd

import jax
import jax.numpy as jnp
from jax import lax
from jax.experimental import pallas as pl
from jax.experimental.pallas import tpu as pltpu
from jax.sharding import PartitionSpec as P

HEADS = 12
HD = 64
BLK = 256
TOK_DEV = 512
CHUNK = 4
epsilon = 1e-05
masked_value = -1e30
bf16 = jnp.bfloat16
f32 = jnp.float32
NT = (((1,), (1,)), ((), ()))
NN = (((1,), (0,)), ((), ()))
TN = (((0,), (0,)), ((), ()))
PARAMS = pltpu.CompilerParams(vmem_limit_bytes=56 * 1024 * 1024)


def dot(a, b, dims=NN):
    return lax.dot_general(a, b, dims, preferred_element_type=f32)


def swap(value, axis, offset):
    size = lax.axis_size(axis)
    return lax.ppermute(value, axis, [(i, i ^ offset) for i in range(size)])


def trade(parts, axis, groups=None):
    return lax.all_to_all(parts, axis, 0, 0, tiled=True, axis_index_groups=groups)


def share(part, count, axis, groups=None):
    return trade(jnp.broadcast_to(part[None], (count,) + part.shape), axis, groups)


def in_order(pieces, index):
    count, bit = len(pieces), 1
    while bit < count:
        odd = (index & bit) != 0
        pieces = [jnp.where(odd, pieces[i ^ bit], pieces[i]) for i in range(count)]
        bit *= 2
    return pieces


def after(value, *others):
    return lax.optimization_barrier((value,) + others)[0]


def norm_stats(values):
    center = jnp.mean(values, axis=-1, keepdims=True)
    offset = values - center
    scale = lax.rsqrt(jnp.mean(offset * offset, axis=-1, keepdims=True) + epsilon)
    return offset * scale, scale


def norm_back(normal, scale, gain, grad):
    inner = grad * gain
    return scale * (
        inner
        - jnp.mean(inner, axis=-1, keepdims=True)
        - normal * jnp.mean(inner * normal, axis=-1, keepdims=True)
    )


def whole(shape):
    return pl.BlockSpec(shape, lambda i, *_: (0,) * len(shape), pipeline_mode=pl.Buffered(1))


def cost(flops, moved, exps=0):
    return pl.CostEstimate(flops=int(flops), bytes_accessed=int(moved), transcendentals=int(exps))


def project_kernel(hidden_ref, wt_ref, vec_ref, out_ref):
    normal, _ = norm_stats(hidden_ref[0].astype(f32))
    normed = (normal * vec_ref[0:1] + vec_ref[1:2]).astype(bf16)
    got = dot(wt_ref[...], normed, NT).astype(bf16)
    span = got.shape[0] // 3
    out_ref[:span, :] = (got[:span].astype(f32) * HD ** (-0.5)).astype(bf16)
    out_ref[span:, :] = got[span:]


def project(hidden, wt, vecs):
    sources, rows, width = hidden.shape
    wide = wt.shape[0]
    return pl.pallas_call(
        project_kernel,
        grid=(sources,),
        in_specs=[
            pl.BlockSpec((1, rows, width), lambda i: (i, 0, 0)),
            whole(wt.shape),
            whole(vecs.shape),
        ],
        out_specs=pl.BlockSpec((wide, rows), lambda i: (0, i)),
        out_shape=jax.ShapeDtypeStruct((wide, sources * rows), bf16),
        compiler_params=PARAMS,
        cost_estimate=cost(2 * sources * rows * width * wide, 4 * sources * rows * width),
        name="project",
    )(hidden, wt, vecs)


def only_head(block, head):
    heads = block.shape[0] // HD
    zero = jnp.zeros((HD, block.shape[1]), block.dtype)
    return jnp.concatenate(
        [block[h * HD : (h + 1) * HD] if h == head else zero for h in range(heads)], axis=0
    )


def key_blocks(number_ref, span, own_ref, far_ref):
    per = own_ref.shape[1] // BLK
    for s in range(1 + far_ref.shape[0]):
        for i in range(per):
            at = pl.multiple_of(number_ref[s * per + i] * BLK, BLK)
            cut = slice(i * BLK, (i + 1) * BLK)
            yield at, (own_ref[span:, cut] if s == 0 else far_ref[s - 1, :, cut])


def attend_kernel(
    number_ref, q_ref, own_ref, far_ref, att_ref, att_t_ref, lse_ref, acc_ref, k_sorted, v_sorted
):
    turn = pl.program_id(0)
    span = acc_ref.shape[0]
    heads = span // HD
    block = number_ref[turn]
    size = CHUNK * BLK

    @pl.when(turn == 0)
    def _():
        for at, kv in key_blocks(number_ref, span, own_ref, far_ref):
            k_sorted[pl.ds(at, BLK), :] = jnp.transpose(kv[:span])
            v_sorted[:, pl.ds(at, BLK)] = kv[span:]

    queries = [only_head(q_ref[...], h) for h in range(heads)]
    acc_ref[...] = jnp.zeros_like(acc_ref)

    def step(last, index, state):
        top, total = state
        at = pl.multiple_of(index * size, size)
        keys = k_sorted[pl.ds(at, size), :]
        tops, totals = [], []
        scores = [dot(keys, queries[h]) for h in range(heads)]
        if last:
            row = lax.broadcasted_iota(jnp.int32, scores[0].shape, 0)
            limit = (block + 1 - index * CHUNK) * BLK
            scores = [jnp.where(row < limit, s, masked_value) for s in scores]
        for h in range(heads):
            rows = slice(h * HD, (h + 1) * HD)
            new_top = jnp.maximum(top[h], jnp.max(scores[h], axis=0, keepdims=True))
            factor = jnp.exp(top[h] - new_top)
            weights = jnp.exp(scores[h] - new_top)
            tops.append(new_top)
            totals.append(total[h] * factor + jnp.sum(weights, axis=0, keepdims=True))
            update = dot(v_sorted[rows, pl.ds(at, size)], weights.astype(bf16))
            acc_ref[rows, :] = acc_ref[rows, :] * factor + update
        return tuple(tops), tuple(totals)

    start = (
        tuple(jnp.full((1, BLK), masked_value, f32) for _ in range(heads)),
        tuple(jnp.zeros((1, BLK), f32) for _ in range(heads)),
    )
    full = (block + 1) // CHUNK
    state = lax.fori_loop(0, full, partial(step, False), start)
    top, total = lax.fori_loop(full, (block + CHUNK) // CHUNK, partial(step, True), state)
    for h in range(heads):
        rows = slice(h * HD, (h + 1) * HD)
        out = acc_ref[rows, :] / total[h]
        att_t_ref[rows, :] = out
        att_ref[0, rows, :] = out.astype(bf16)
        lse_ref[0, h : h + 1, :] = top[h] + jnp.log(total[h])


def attend(numbers, own, far):
    span, rows = own.shape[0] // 3, own.shape[1]
    blocks = rows // BLK
    keys = rows * (1 + far.shape[0])
    return pl.pallas_call(
        attend_kernel,
        grid_spec=pltpu.PrefetchScalarGridSpec(
            num_scalar_prefetch=1,
            grid=(blocks,),
            in_specs=[
                pl.BlockSpec((span, BLK), lambda i, *_: (0, i)),
                whole(own.shape),
                whole(far.shape),
            ],
            out_specs=[
                pl.BlockSpec((1, span, BLK), lambda i, *_: (i // 2, 0, i % 2)),
                pl.BlockSpec((span, BLK), lambda i, *_: (0, i)),
                pl.BlockSpec((1, 8, BLK), lambda i, *_: (i, 0, 0)),
            ],
            scratch_shapes=[
                pltpu.VMEM((span, BLK), f32),
                pltpu.VMEM((keys, span), bf16),
                pltpu.VMEM((span, keys), bf16),
            ],
        ),
        out_shape=[
            jax.ShapeDtypeStruct((blocks // 2, span, 2 * BLK), bf16),
            jax.ShapeDtypeStruct((span, rows), f32),
            jax.ShapeDtypeStruct((blocks, 8, BLK), f32),
        ],
        compiler_params=PARAMS,
        cost_estimate=cost(12 * rows * keys * span, 8 * keys * span, rows * keys * span // 128),
        name="attend",
    )(numbers, own, own, far)


def attend_back_kernel(
    number_ref, q_ref, g_ref, att_t_ref, lse_ref, own_ref, far_ref, gq_ref, gown_ref, gfar_ref,
    gq_acc, gk_acc, gv_acc, k_sorted, v_sorted, kt_sorted,
):
    turn = pl.program_id(0)
    span = gq_acc.shape[0]
    heads = span // HD
    block = number_ref[turn]
    size = CHUNK * BLK

    @pl.when(turn == 0)
    def _():
        gk_acc[...] = jnp.zeros_like(gk_acc)
        gv_acc[...] = jnp.zeros_like(gv_acc)
        for at, kv in key_blocks(number_ref, span, own_ref, far_ref):
            k_sorted[pl.ds(at, BLK), :] = jnp.transpose(kv[:span])
            v_sorted[pl.ds(at, BLK), :] = jnp.transpose(kv[span:])
            kt_sorted[:, pl.ds(at, BLK)] = kv[:span]

    grads = g_ref[0]
    prod = grads.astype(f32) * att_t_ref[...]
    part = lambda h: slice(h * HD, (h + 1) * HD)
    deltas = [jnp.sum(prod[part(h)], axis=0, keepdims=True) for h in range(heads)]
    logs = [lse_ref[0, h : h + 1, :] for h in range(heads)]
    q_only = [only_head(q_ref[...], h) for h in range(heads)]
    g_only = [only_head(grads, h) for h in range(heads)]
    gq_acc[...] = jnp.zeros_like(gq_acc)

    def step(last, index, carry):
        at = pl.multiple_of(index * size, size)
        keys = k_sorted[pl.ds(at, size), :]
        values = v_sorted[pl.ds(at, size), :]
        if last:
            row = lax.broadcasted_iota(jnp.int32, (size, BLK), 0)
            allowed = row < (block + 1 - index * CHUNK) * BLK
        for h in range(heads):
            rows = part(h)
            probs = jnp.exp(dot(keys, q_only[h]) - logs[h])
            if last:
                probs = jnp.where(allowed, probs, 0.0)
            gs = (probs * (dot(values, g_only[h]) - deltas[h])).astype(bf16)
            gq_acc[rows, :] += dot(kt_sorted[rows, pl.ds(at, size)], gs)
            gv_acc[rows, pl.ds(at, size)] += dot(grads[rows], probs.astype(bf16), NT)
            gk_acc[rows, pl.ds(at, size)] += dot(q_ref[rows, :], gs, NT)
        return carry

    full = (block + 1) // CHUNK
    lax.fori_loop(0, full, partial(step, False), 0)
    lax.fori_loop(full, (block + CHUNK) // CHUNK, partial(step, True), 0)
    gq_ref[...] = (gq_acc[...] * HD ** (-0.5)).astype(bf16)

    @pl.when(turn == pl.num_programs(0) - 1)
    def _():
        per = own_ref.shape[1] // BLK
        for s in range(1 + far_ref.shape[0]):
            for i in range(per):
                at = pl.multiple_of(number_ref[s * per + i] * BLK, BLK)
                cut = slice(i * BLK, (i + 1) * BLK)
                gk = gk_acc[:, pl.ds(at, BLK)].astype(bf16)
                gv = gv_acc[:, pl.ds(at, BLK)].astype(bf16)
                if s == 0:
                    gown_ref[:span, cut], gown_ref[span:, cut] = gk, gv
                else:
                    gfar_ref[s - 1, :span, cut], gfar_ref[s - 1, span:, cut] = gk, gv


def attend_back(numbers, own, far, grads, att_t, logs):
    span, rows = own.shape[0] // 3, own.shape[1]
    blocks = rows // BLK
    keys = rows * (1 + far.shape[0])
    column = pl.BlockSpec((span, BLK), lambda i, *_: (0, i))
    return pl.pallas_call(
        attend_back_kernel,
        grid_spec=pltpu.PrefetchScalarGridSpec(
            num_scalar_prefetch=1,
            grid=(blocks,),
            in_specs=[
                column,
                pl.BlockSpec((1, span, BLK), lambda i, *_: (i // 2, 0, i % 2)),
                column,
                pl.BlockSpec((1, 8, BLK), lambda i, *_: (i, 0, 0)),
                whole(own.shape),
                whole(far.shape),
            ],
            out_specs=[column, whole((2 * span, rows)), whole(far.shape)],
            scratch_shapes=[
                pltpu.VMEM((span, BLK), f32),
                pltpu.VMEM((span, keys), f32),
                pltpu.VMEM((span, keys), f32),
                pltpu.VMEM((keys, span), bf16),
                pltpu.VMEM((keys, span), bf16),
                pltpu.VMEM((span, keys), bf16),
            ],
        ),
        out_shape=[
            jax.ShapeDtypeStruct((span, rows), bf16),
            jax.ShapeDtypeStruct((2 * span, rows), bf16),
            jax.ShapeDtypeStruct(far.shape, bf16),
        ],
        compiler_params=PARAMS,
        cost_estimate=cost(30 * rows * keys * span, 16 * keys * span, rows * keys * span // 128),
        name="attend_back",
    )(numbers, own, grads, att_t, logs, own, far)


def middle_kernel(att_ref, x_ref, w_ref, vec_ref, slot_ref, mid_ref, normed_ref, send_ref):
    middle = x_ref[...].astype(f32) + dot(att_ref[...], w_ref[...], TN)
    normal, _ = norm_stats(middle)
    normed = (normal * vec_ref[2:3] + vec_ref[3:4]).astype(bf16)
    mid_ref[...] = middle
    normed_ref[...] = normed
    slots = lax.broadcasted_iota(jnp.int32, (send_ref.shape[0], x_ref.shape[0]), 0)
    place = (slots == slot_ref[...]).astype(f32).astype(bf16)
    send_ref[...] = dot(place, normed).astype(bf16)


def middle_step(att_t, rows, weight, vecs, slot, all_slots):
    count, width = rows.shape
    return pl.pallas_call(
        middle_kernel,
        out_shape=[
            jax.ShapeDtypeStruct((count, width), f32),
            jax.ShapeDtypeStruct((count, width), bf16),
            jax.ShapeDtypeStruct((all_slots, width), bf16),
        ],
        compiler_params=PARAMS,
        cost_estimate=cost(2 * count * width * (width + all_slots), 10 * count * width),
        name="middle",
    )(att_t, rows, weight, vecs, slot[None, :])


def turn_kernel(
    got_ref, far_ref, slot_ref, mid_ref, cot_ref, w_ref, vec_ref, gmid_ref, gbr_ref, gatt_ref, sum_ref
):
    slots = lax.broadcasted_iota(jnp.int32, (mid_ref.shape[0], got_ref.shape[0]), 1)
    place = (slots == slot_ref[...]).astype(f32).astype(bf16)
    grad = (dot(place, got_ref[...]) + far_ref[...].astype(f32)).astype(bf16).astype(f32)
    normal, scale = norm_stats(mid_ref[...])
    middle = cot_ref[...].astype(f32) + norm_back(normal, scale, vec_ref[2:3], grad)
    branch = middle.astype(bf16)
    gmid_ref[...] = middle
    gbr_ref[...] = branch
    gatt_ref[...] = dot(w_ref[...], branch, NT).astype(bf16)
    sum_ref[...] = jnp.zeros_like(sum_ref)
    sum_ref[0:1] = jnp.sum(grad * normal, axis=0, keepdims=True)
    sum_ref[1:2] = jnp.sum(grad, axis=0, keepdims=True)


def turn_step(got, far, slot, middle, cot, weight, vecs):
    count, width = middle.shape
    return pl.pallas_call(
        turn_kernel,
        out_shape=[
            jax.ShapeDtypeStruct((count, width), f32),
            jax.ShapeDtypeStruct((count, width), bf16),
            jax.ShapeDtypeStruct((weight.shape[0], count), bf16),
            jax.ShapeDtypeStruct((128, width), f32),
        ],
        compiler_params=PARAMS,
        cost_estimate=cost(2 * count * width * (width + got.shape[0]), 12 * count * width),
        name="turn",
    )(got, far, slot[:, None], middle, cot, weight, vecs)


def out_grad_kernel(att_ref, gbr_ref, sum_ref, out_ref):
    width = gbr_ref.shape[1]
    out_ref[:, :width] = dot(att_ref[...], gbr_ref[...]).astype(bf16)
    out_ref[:, width:] = jnp.transpose(sum_ref[...]).astype(bf16)


def out_grad_step(att_t, gbr, sums):
    return pl.pallas_call(
        out_grad_kernel,
        out_shape=jax.ShapeDtypeStruct((att_t.shape[0], gbr.shape[1] + 128), bf16),
        compiler_params=PARAMS,
        cost_estimate=cost(2 * att_t.size * gbr.shape[1], 6 * gbr.size),
        name="out_grad",
    )(att_t, gbr, sums)


def tail_kernel(
    gq_ref, gown_ref, got_ref, hidden_ref, wt_ref, vec_ref, rows_ref, mixed_ref, gw_acc, sum_acc
):
    turn = pl.program_id(0)

    @pl.when(turn == 0)
    def _():
        gw_acc[...] = jnp.zeros_like(gw_acc)
        sum_acc[...] = jnp.zeros_like(sum_acc)

    gkv = gown_ref[...].astype(f32)
    for k in range(got_ref.shape[0]):
        gkv = gkv + got_ref[k].astype(f32)
    columns = jnp.concatenate([gq_ref[...], gkv.astype(bf16)], axis=0)
    rows = dot(columns, wt_ref[...], TN)
    rows_ref[0] = rows.astype(bf16)
    normal, _ = norm_stats(hidden_ref[0].astype(f32))
    normed = (normal * vec_ref[0:1] + vec_ref[1:2]).astype(bf16)
    sum_acc[0:1] += jnp.sum(rows * normal, axis=0, keepdims=True)
    sum_acc[1:2] += jnp.sum(rows, axis=0, keepdims=True)
    gw_acc[...] += dot(columns, normed)

    @pl.when(turn == pl.num_programs(0) - 1)
    def _():
        cores, planes, count, _ = mixed_ref.shape
        wide = gw_acc.shape[0]
        weights = jnp.transpose(gw_acc[...]).astype(bf16)
        sums = jnp.transpose(sum_acc[...]).astype(bf16)
        for z in range(planes):
            for s in range(cores):
                at = (z * cores + s) * count
                mixed_ref[s, z, :, :wide] = weights[at : at + count]
                mixed_ref[s, z, :, wide:] = sums[at : at + count]


def tail_step(gq, gown, got, hidden, wt, vecs, cores, planes):
    sources, rows, width = hidden.shape
    wide = wt.shape[0]
    count = width // (cores * planes)
    return pl.pallas_call(
        tail_kernel,
        grid=(sources,),
        in_specs=[
            pl.BlockSpec((gq.shape[0], rows), lambda i: (0, i)),
            pl.BlockSpec((gown.shape[0], rows), lambda i: (0, i)),
            pl.BlockSpec((got.shape[0], gown.shape[0], rows), lambda i: (0, 0, i)),
            pl.BlockSpec((1, rows, width), lambda i: (i, 0, 0)),
            whole(wt.shape),
            whole(vecs.shape),
        ],
        out_specs=[
            pl.BlockSpec((1, rows, width), lambda i: (i, 0, 0)),
            whole((cores, planes, count, wide + 128)),
        ],
        out_shape=[
            jax.ShapeDtypeStruct((sources, rows, width), bf16),
            jax.ShapeDtypeStruct((cores, planes, count, wide + 128), bf16),
        ],
        scratch_shapes=[pltpu.VMEM((wide, width), f32), pltpu.VMEM((128, width), f32)],
        compiler_params=PARAMS,
        cost_estimate=cost(4 * sources * rows * width * wide, 6 * sources * rows * width),
        name="tail",
    )(gq, gown, got, hidden, wt, vecs)


def assemble_kernel(span, groups, part_ref, out_ref, sum_ref):
    count, rows, _ = part_ref.shape
    cores = count // groups
    for s in range(cores):
        at = slice(s * rows, (s + 1) * rows)
        pieces = [part_ref[g * cores + s].astype(f32) for g in range(groups)]
        out_ref[at, :] = jnp.concatenate(
            [p[:, t * span : (t + 1) * span] for t in range(3) for p in pieces], axis=1
        )
        sum_ref[at, :] = sum(p[:, 3 * span :] for p in pieces)


def assemble(part, span, groups):
    count, rows, wide = part.shape
    total = rows * (count // groups)
    return pl.pallas_call(
        partial(assemble_kernel, span, groups),
        out_shape=[
            jax.ShapeDtypeStruct((total, 3 * span * groups), f32),
            jax.ShapeDtypeStruct((total, wide - 3 * span), f32),
        ],
        compiler_params=PARAMS,
        cost_estimate=cost(part.size, 6 * part.size),
        name="assemble",
    )(part)


def expert_kernel(x_ref, gy_ref, first_ref, second_ref, act_ref, gpre_ref, gn_ref, ey_ref):
    flat = lambda ref: ref[...].reshape(-1, ref.shape[-1])
    first, second = first_ref[0], second_ref[0]
    pre = dot(flat(x_ref), first)
    inner = 0.7978845608028654 * (pre + 0.044715 * (pre * pre * pre))
    bend = jnp.tanh(inner)
    half = 0.5 * (1.0 + bend)
    act = (pre * half).astype(bf16)
    slope = half + 0.5 * pre * (1.0 - bend * bend) * (
        0.7978845608028654 * (1.0 + 3 * 0.044715 * (pre * pre))
    )
    gpre = (dot(flat(gy_ref), second) * slope).astype(bf16)
    act_ref[...] = act.reshape(act_ref.shape)
    gpre_ref[...] = gpre.reshape(gpre_ref.shape)
    gn_ref[...] = dot(gpre, first, NT).astype(bf16).reshape(gn_ref.shape)
    ey_ref[...] = dot(act, second, NT).astype(bf16).reshape(ey_ref.shape)


def expert_step(tokens, grads, first, second):
    sources, experts, room, width = tokens.shape
    hidden = first.shape[2]
    token_spec = pl.BlockSpec((sources, 1, room, width), lambda e: (0, e, 0, 0))
    hidden_spec = pl.BlockSpec((sources, 1, room, hidden), lambda e: (0, e, 0, 0))
    weight_spec = pl.BlockSpec((1, width, hidden), lambda e: (e, 0, 0))
    like = lambda last: jax.ShapeDtypeStruct((sources, experts, room, last), bf16)
    return pl.pallas_call(
        expert_kernel,
        grid=(experts,),
        in_specs=[token_spec, token_spec, weight_spec, weight_spec],
        out_specs=[hidden_spec, hidden_spec, token_spec, token_spec],
        out_shape=[like(hidden), like(hidden), like(width), like(width)],
        compiler_params=PARAMS,
        cost_estimate=pl.CostEstimate(
            flops=8 * sources * experts * room * width * hidden,
            bytes_accessed=4 * first.size + 12 * tokens.size,
            transcendentals=sources * experts * room * hidden,
        ),
        name="expert_step",
    )(tokens, grads, first, second)


def expert_grad_kernel(parts, *refs):
    flat = lambda ref: ref[...].reshape(-1, ref.shape[-1])
    stack = lambda some: jnp.concatenate([flat(r) for r in some], axis=0)
    ins, (gfirst_ref, gsecond_ref) = refs[: 4 * parts], refs[4 * parts :]
    tokens, grads, acts, gpres = (stack(ins[i * parts : (i + 1) * parts]) for i in range(4))
    gfirst_ref[0] = dot(tokens, gpres, TN)
    gsecond_ref[0] = dot(grads, acts, TN)


def expert_grads(tokens, grads, acts, gpres):
    parts = len(tokens)
    sources, experts, room, width = tokens[0].shape
    hidden = acts[0].shape[3]
    spec = lambda last: pl.BlockSpec((sources, 1, room, last), lambda e: (0, e, 0, 0))
    out_spec = pl.BlockSpec((1, width, hidden), lambda e: (e, 0, 0))
    out = jax.ShapeDtypeStruct((experts, width, hidden), f32)
    return pl.pallas_call(
        partial(expert_grad_kernel, parts),
        grid=(experts,),
        in_specs=[spec(width)] * (2 * parts) + [spec(hidden)] * (2 * parts),
        out_specs=[out_spec, out_spec],
        out_shape=[out, out],
        compiler_params=PARAMS,
        cost_estimate=pl.CostEstimate(
            flops=4 * parts * sources * experts * room * width * hidden,
            bytes_accessed=8 * experts * width * hidden,
            transcendentals=0,
        ),
        name="expert_grads",
    )(*tokens, *grads, *acts, *gpres)


def local(
    hidden_in, token_ids, hash_table, deal_order, qkv_weight, out_weight,
    norm1_gain, norm1_bias, norm2_gain, norm2_bias, expert_in, expert_out, out_grad,
):
    devices = lax.axis_size("ctx")
    position = lax.axis_index("ctx")
    planes = lax.axis_size("fsdp")
    plane = lax.axis_index("fsdp")
    width = hidden_in.shape[2]
    local_experts = expert_in.shape[0]
    experts = local_experts * devices
    room = 2 * TOK_DEV // experts
    all_slots = experts * room
    groups = gcd(HEADS, devices)
    cores = devices // groups
    group, core = position // cores, position % cores
    span = width // groups
    across = [[g * cores + c for g in range(groups)] for c in range(cores)]

    own_hidden = hidden_in[0]
    out_cot = out_grad[0]

    hidden = share(own_hidden, groups, "ctx", across).reshape(groups, TOK_DEV, width)
    cut = lambda part: lax.dynamic_slice_in_dim(qkv_weight, part * width + group * span, span, 1)
    vecs = jnp.stack([norm1_gain, norm1_bias, norm2_gain, norm2_bias], axis=1)
    own_cols = jnp.concatenate(
        [cut(0), cut(1), cut(2), jnp.pad(vecs, ((0, 0), (0, 60))), out_weight], axis=1
    )
    full = lax.all_gather(own_cols, "fsdp", axis=0, tiled=True)
    wt, out_full = full[:, : 3 * span].T, full[:, 3 * span + 64 :]
    vecs = full[:, 3 * span : 3 * span + 4].T.astype(f32)

    expert_of = hash_table[token_ids[0]]
    same = expert_of[:, None] == expert_of[None, :]
    shape = (TOK_DEV, TOK_DEV)
    before = lax.broadcasted_iota(jnp.int32, shape, 1) < lax.broadcasted_iota(jnp.int32, shape, 0)
    slot = expert_of * room + jnp.sum((same & before).astype(jnp.int32), axis=1)

    def spread(value):
        far = [None, None]
        for k in range(2, planes):
            far.append(swap(far[k - 1], "fsdp", 1) if k % 2 else swap(value, "fsdp", k))
        return far

    far_slots = spread(slot)
    counter = lambda axis: lax.broadcasted_iota(
        jnp.int32, (all_slots, TOK_DEV) if axis == 0 else (TOK_DEV, all_slots), axis
    )
    place = lambda s, rows: dot((counter(0) == s[None, :]).astype(bf16), rows).astype(bf16)
    fetch = lambda s, rows: dot((counter(1) == s[:, None]).astype(bf16), rows)
    shaped = (devices, local_experts, room, width)
    exchange = lambda rows: trade(
        rows.reshape(devices, local_experts * room, width), "ctx"
    ).reshape(shaped)

    evens = range(2, planes, 2)
    far_cots = {k: swap(out_cot, "fsdp", k) for k in evens}
    gys = [exchange(after(place(slot, out_cot), hidden))]
    gys.append(swap(gys[0], "fsdp", 1))
    for k in evens:
        gys.append(exchange(place(far_slots[k], far_cots[k])))
        gys.append(swap(gys[k], "fsdp", 1))

    own = project(hidden, wt, vecs)
    far = jnp.stack([swap(own[span:], "ctx", k) for k in range(1, cores)])
    order = deal_order.reshape(groups, cores)
    low = jnp.stack([lax.dynamic_index_in_dim(order, core ^ s, 1, False) for s in range(cores)])
    numbers = jnp.stack([low, 2 * devices - 1 - low], axis=2).reshape(-1)
    att, att_f, logs = attend(numbers, own, far)
    att_t = trade(att, "ctx", across).reshape(width, TOK_DEV)
    middle, normed, sent = middle_step(att_t, own_hidden, out_full, vecs, slot, all_slots)

    far_rows = spread(normed)
    tokens = [exchange(sent)]
    tokens.append(swap(tokens[0], "fsdp", 1))
    for k in range(2, planes):
        tokens.append(exchange(place(far_slots[k], far_rows[k])))
    acts, gpres, gns, eys = [], [], [], []
    for k in range(planes):
        act, gpre, gn, ey = expert_step(tokens[k], gys[k], expert_in, expert_out)
        acts.append(act)
        gpres.append(gpre)
        gns.append(gn)
        eys.append(ey)

    far_grad = jnp.zeros((TOK_DEV, width), f32)
    for k in evens:
        last = fetch(far_slots[k + 1], exchange(gns[k + 1]).reshape(all_slots, width)).astype(bf16)
        back = fetch(far_slots[k], exchange(gns[k]).reshape(all_slots, width))
        back = (back + swap(last, "fsdp", 1).astype(f32)).astype(bf16)
        far_grad = far_grad + swap(back, "fsdp", k).astype(f32)
    near = (gns[0].astype(f32) + swap(gns[1], "fsdp", 1).astype(f32)).astype(bf16)
    near = exchange(near).reshape(all_slots, width)
    grad_middle, branch, gatt, sums_two = turn_step(
        near, far_grad.astype(bf16), slot, middle, out_cot, out_full, vecs
    )
    gatt = trade(gatt.reshape(groups, span, TOK_DEV), "ctx", across)
    outs = out_grad_step(att_t, branch, sums_two)
    grad_expert_in, grad_expert_out = expert_grads(tokens, gys, acts, gpres)

    total_y = eys[0].astype(f32) + swap(eys[1], "fsdp", 1).astype(f32)
    for k in evens:
        back = (eys[k].astype(f32) + swap(eys[k + 1], "fsdp", 1).astype(f32)).astype(bf16)
        total_y = total_y + swap(back, "fsdp", k).astype(f32)
    token_y = fetch(slot, exchange(total_y.astype(bf16)).reshape(all_slots, width))
    layer_out = (middle + token_y).astype(bf16)

    gq, gown, gfar = attend_back(numbers, own, far, gatt, att_f, logs)
    got = jnp.stack([swap(gfar[k - 1], "ctx", k) for k in range(1, cores)])
    grad_rows, mixed = tail_step(gq, gown, got, hidden, wt, vecs, cores, planes)
    grad_rows = trade(grad_rows, "ctx", across)
    grad_normed = jnp.sum(grad_rows.astype(f32), axis=0)
    own_normal, own_scale = norm_stats(own_hidden.astype(f32))
    grad_hidden = grad_middle + norm_back(own_normal, own_scale, vecs[0], grad_normed)

    def keep(parts, index, axis, stride):
        pick = lambda k: lax.dynamic_index_in_dim(parts, index ^ k, 0, False)
        total = pick(0).astype(f32)
        for k in range(1, parts.shape[0]):
            total = total + swap(pick(k), axis, k * stride).astype(f32)
        return total.astype(bf16)

    def collect(part):
        pieces = [part] + [swap(part, "ctx", j * cores) for j in range(1, groups)]
        mine = jnp.stack(in_order(pieces, group))
        sides = in_order([mine] + [swap(mine, "ctx", k) for k in range(1, cores)], core)
        return jnp.stack(sides, axis=1).reshape((devices,) + part.shape)

    part = keep(keep(mixed, core, "ctx", 1), plane, "fsdp", 1)
    grad_qkv, vec_one = assemble(collect(part), span, groups)

    rows = width // planes
    wide = outs.shape[1]
    part = jnp.moveaxis(outs.reshape(planes, devices, rows // devices, wide), 1, 0)
    part = jnp.sum(trade(part, "ctx").astype(f32), axis=0).astype(bf16)
    part = keep(part, plane, "fsdp", 1)
    part = share(part, devices, "ctx").reshape(rows, wide).astype(f32)
    return (
        layer_out[None],
        grad_hidden[None],
        grad_qkv,
        part[:, :width],
        vec_one[:, 0],
        vec_one[:, 1],
        part[:, width],
        part[:, width + 1],
        grad_expert_in,
        grad_expert_out,
    )


def solution(mesh):
    return jax.shard_map(
        local,
        mesh=mesh,
        in_specs=(
            P("fsdp", "ctx", None),
            P("fsdp", "ctx"),
            P(),
            P(),
            P("fsdp", None),
            P("fsdp", None),
            P("fsdp"),
            P("fsdp"),
            P("fsdp"),
            P("fsdp"),
            P("ctx", None, "fsdp"),
            P("ctx", None, "fsdp"),
            P("fsdp", "ctx", None),
        ),
        out_specs=(
            P("fsdp", "ctx", None),
            P("fsdp", "ctx", None),
            P("fsdp", None),
            P("fsdp", None),
            P("fsdp"),
            P("fsdp"),
            P("fsdp"),
            P("fsdp"),
            P("ctx", None, "fsdp"),
            P("ctx", None, "fsdp"),
        ),
        check_vma=False,
    )
```

```python
from functools import partial
from math import gcd

import jax
import jax.numpy as jnp
from jax import lax
from jax.experimental import pallas as pl
from jax.experimental.pallas import tpu as pltpu
from jax.sharding import PartitionSpec as P

HEADS = 12
HD = 64
BLK = 256
TOK_DEV = 512
CHUNK = 4
epsilon = 1e-05
masked_value = -1e30
bf16 = jnp.bfloat16
f32 = jnp.float32
NT = (((1,), (1,)), ((), ()))
NN = (((1,), (0,)), ((), ()))
TN = (((0,), (0,)), ((), ()))
PARAMS = pltpu.CompilerParams(vmem_limit_bytes=56 * 1024 * 1024)


def dot(a, b, dims=NN):
    return lax.dot_general(a, b, dims, preferred_element_type=f32)


def swap(value, axis, offset):
    size = lax.axis_size(axis)
    return lax.ppermute(value, axis, [(i, i ^ offset) for i in range(size)])


def trade(parts, axis, groups=None):
    return lax.all_to_all(parts, axis, 0, 0, tiled=True, axis_index_groups=groups)


def share(part, count, axis, groups=None):
    return trade(jnp.broadcast_to(part[None], (count,) + part.shape), axis, groups)


def in_order(pieces, index):
    count, bit = len(pieces), 1
    while bit < count:
        odd = (index & bit) != 0
        pieces = [jnp.where(odd, pieces[i ^ bit], pieces[i]) for i in range(count)]
        bit *= 2
    return pieces


def after(value, *others):
    return lax.optimization_barrier((value,) + others)[0]


def norm_stats(values):
    center = jnp.mean(values, axis=-1, keepdims=True)
    offset = values - center
    scale = lax.rsqrt(jnp.mean(offset * offset, axis=-1, keepdims=True) + epsilon)
    return offset * scale, scale


def norm_back(normal, scale, gain, grad):
    inner = grad * gain
    return scale * (
        inner
        - jnp.mean(inner, axis=-1, keepdims=True)
        - normal * jnp.mean(inner * normal, axis=-1, keepdims=True)
    )


def whole(shape):
    return pl.BlockSpec(shape, lambda i, *_: (0,) * len(shape), pipeline_mode=pl.Buffered(1))


def cost(flops, moved, exps=0):
    return pl.CostEstimate(flops=int(flops), bytes_accessed=int(moved), transcendentals=int(exps))


def project_kernel(hidden_ref, wt_ref, vec_ref, out_ref):
    normal, _ = norm_stats(hidden_ref[...].astype(f32))
    normed = (normal * vec_ref[0:1] + vec_ref[1:2]).astype(bf16)
    got = dot(wt_ref[...], normed, NT).astype(bf16)
    span = got.shape[0] // 3
    out_ref[:span, :] = (got[:span].astype(f32) * HD ** (-0.5)).astype(bf16)
    out_ref[span:, :] = got[span:]


def project(hidden, wt, vecs):
    rows, width = hidden.shape
    wide = wt.shape[0]
    return pl.pallas_call(
        project_kernel,
        out_shape=jax.ShapeDtypeStruct((wide, rows), bf16),
        compiler_params=PARAMS,
        cost_estimate=cost(2 * rows * width * wide, 4 * rows * width),
        name="project",
    )(hidden, wt, vecs)


def only_head(block, head):
    heads = block.shape[0] // HD
    zero = jnp.zeros((HD, block.shape[1]), block.dtype)
    return jnp.concatenate(
        [block[h * HD : (h + 1) * HD] if h == head else zero for h in range(heads)], axis=0
    )


def key_blocks(number_ref, own_refs, far_refs):
    span = own_refs[0].shape[0] // 3
    per = own_refs[0].shape[1] // BLK
    for p, ref in enumerate(own_refs + far_refs):
        for i in range(per):
            at = pl.multiple_of(number_ref[p * per + i] * BLK, BLK)
            cut = slice(i * BLK, (i + 1) * BLK)
            yield at, (ref[span:, cut] if p < len(own_refs) else ref[:, cut])


def attend_kernel(pieces, sides, number_ref, order_ref, *refs):
    own_refs, far_refs = refs[:pieces], refs[pieces : pieces * sides]
    att_ref, att_t_ref, lse_ref, acc_ref, q_all, k_sorted, v_sorted = refs[pieces * sides :]
    turn = pl.program_id(0)
    span = acc_ref.shape[0]
    heads = span // HD
    block = number_ref[turn]
    size = CHUNK * BLK

    @pl.when(turn == 0)
    def _():
        for p, ref in enumerate(own_refs):
            rows = ref.shape[1]
            q_all[:, p * rows : (p + 1) * rows] = ref[:span, :]
        for at, kv in key_blocks(number_ref, own_refs, far_refs):
            k_sorted[pl.ds(at, BLK), :] = jnp.transpose(kv[:span])
            v_sorted[:, pl.ds(at, BLK)] = kv[span:]

    own_queries = q_all[:, pl.ds(pl.multiple_of(turn * BLK, BLK), BLK)]
    queries = [only_head(own_queries, h) for h in range(heads)]
    acc_ref[...] = jnp.zeros_like(acc_ref)

    def step(last, index, state):
        top, total = state
        at = pl.multiple_of(index * size, size)
        keys = k_sorted[pl.ds(at, size), :]
        tops, totals = [], []
        scores = [dot(keys, queries[h]) for h in range(heads)]
        if last:
            row = lax.broadcasted_iota(jnp.int32, scores[0].shape, 0)
            limit = (block + 1 - index * CHUNK) * BLK
            scores = [jnp.where(row < limit, s, masked_value) for s in scores]
        for h in range(heads):
            rows = slice(h * HD, (h + 1) * HD)
            new_top = jnp.maximum(top[h], jnp.max(scores[h], axis=0, keepdims=True))
            factor = jnp.exp(top[h] - new_top)
            weights = jnp.exp(scores[h] - new_top)
            tops.append(new_top)
            totals.append(total[h] * factor + jnp.sum(weights, axis=0, keepdims=True))
            update = dot(v_sorted[rows, pl.ds(at, size)], weights.astype(bf16))
            acc_ref[rows, :] = acc_ref[rows, :] * factor + update
        return tuple(tops), tuple(totals)

    start = (
        tuple(jnp.full((1, BLK), masked_value, f32) for _ in range(heads)),
        tuple(jnp.zeros((1, BLK), f32) for _ in range(heads)),
    )
    full = (block + 1) // CHUNK
    state = lax.fori_loop(0, full, partial(step, False), start)
    top, total = lax.fori_loop(full, (block + CHUNK) // CHUNK, partial(step, True), state)
    for h in range(heads):
        rows = slice(h * HD, (h + 1) * HD)
        out = acc_ref[rows, :] / total[h]
        att_t_ref[rows, :] = out
        att_ref[0, rows, :] = out.astype(bf16)
        lse_ref[0, h : h + 1, :] = top[h] + jnp.log(total[h])


def attend(numbers, order, own, far):
    pieces, sides = len(own), 1 + len(far) // len(own)
    span, piece = own[0].shape[0] // 3, own[0].shape[1]
    rows = pieces * piece
    blocks = rows // BLK
    keys = rows * sides
    return pl.pallas_call(
        partial(attend_kernel, pieces, sides),
        grid_spec=pltpu.PrefetchScalarGridSpec(
            num_scalar_prefetch=2,
            grid=(blocks,),
            in_specs=[whole(a.shape) for a in own + far],
            out_specs=[
                pl.BlockSpec((1, span, BLK), lambda i, n, o: (o[i // 2], 0, i % 2)),
                pl.BlockSpec((span, BLK), lambda i, *_: (0, i)),
                pl.BlockSpec((1, 8, BLK), lambda i, *_: (i, 0, 0)),
            ],
            scratch_shapes=[
                pltpu.VMEM((span, BLK), f32),
                pltpu.VMEM((span, rows), bf16),
                pltpu.VMEM((keys, span), bf16),
                pltpu.VMEM((span, keys), bf16),
            ],
        ),
        out_shape=[
            jax.ShapeDtypeStruct((pieces, span, piece), bf16),
            jax.ShapeDtypeStruct((span, rows), f32),
            jax.ShapeDtypeStruct((blocks, 8, BLK), f32),
        ],
        compiler_params=PARAMS,
        cost_estimate=cost(12 * rows * keys * span, 8 * keys * span, rows * keys * span // 128),
        name="attend",
    )(numbers, order, *own, *far)


def attend_back_kernel(pieces, sides, number_ref, order_ref, g_ref, att_t_ref, lse_ref, *refs):
    own_refs, far_refs = refs[:pieces], refs[pieces : pieces * sides]
    gq_ref, gown_ref, gfar_ref = refs[pieces * sides : pieces * sides + 3]
    gq_acc, gk_acc, gv_acc, q_all, k_sorted, v_sorted, kt_sorted = refs[pieces * sides + 3 :]
    turn = pl.program_id(0)
    span = gq_acc.shape[0]
    heads = span // HD
    block = number_ref[turn]
    size = CHUNK * BLK

    @pl.when(turn == 0)
    def _():
        gk_acc[...] = jnp.zeros_like(gk_acc)
        gv_acc[...] = jnp.zeros_like(gv_acc)
        for p, ref in enumerate(own_refs):
            rows = ref.shape[1]
            q_all[:, p * rows : (p + 1) * rows] = ref[:span, :]
        for at, kv in key_blocks(number_ref, own_refs, far_refs):
            k_sorted[pl.ds(at, BLK), :] = jnp.transpose(kv[:span])
            v_sorted[pl.ds(at, BLK), :] = jnp.transpose(kv[span:])
            kt_sorted[:, pl.ds(at, BLK)] = kv[:span]

    grads = g_ref[0]
    queries = q_all[:, pl.ds(pl.multiple_of(turn * BLK, BLK), BLK)]
    prod = grads.astype(f32) * att_t_ref[...]
    part = lambda h: slice(h * HD, (h + 1) * HD)
    deltas = [jnp.sum(prod[part(h)], axis=0, keepdims=True) for h in range(heads)]
    logs = [lse_ref[0, h : h + 1, :] for h in range(heads)]
    q_only = [only_head(queries, h) for h in range(heads)]
    g_only = [only_head(grads, h) for h in range(heads)]
    gq_acc[...] = jnp.zeros_like(gq_acc)

    def step(last, index, carry):
        at = pl.multiple_of(index * size, size)
        keys = k_sorted[pl.ds(at, size), :]
        values = v_sorted[pl.ds(at, size), :]
        if last:
            row = lax.broadcasted_iota(jnp.int32, (size, BLK), 0)
            allowed = row < (block + 1 - index * CHUNK) * BLK
        for h in range(heads):
            rows = part(h)
            probs = jnp.exp(dot(keys, q_only[h]) - logs[h])
            if last:
                probs = jnp.where(allowed, probs, 0.0)
            gs = (probs * (dot(values, g_only[h]) - deltas[h])).astype(bf16)
            gq_acc[rows, :] += dot(kt_sorted[rows, pl.ds(at, size)], gs)
            gv_acc[rows, pl.ds(at, size)] += dot(grads[rows], probs.astype(bf16), NT)
            gk_acc[rows, pl.ds(at, size)] += dot(queries[rows], gs, NT)
        return carry

    full = (block + 1) // CHUNK
    lax.fori_loop(0, full, partial(step, False), 0)
    lax.fori_loop(full, (block + CHUNK) // CHUNK, partial(step, True), 0)
    gq_ref[...] = (gq_acc[...] * HD ** (-0.5)).astype(bf16)

    @pl.when(turn == pl.num_programs(0) - 1)
    def _():
        per = gown_ref.shape[1] // BLK
        for s in range(sides):
            for i in range(per):
                at = pl.multiple_of(number_ref[s * per + i] * BLK, BLK)
                cut = slice(i * BLK, (i + 1) * BLK)
                gk = gk_acc[:, pl.ds(at, BLK)].astype(bf16)
                gv = gv_acc[:, pl.ds(at, BLK)].astype(bf16)
                if s == 0:
                    gown_ref[:span, cut], gown_ref[span:, cut] = gk, gv
                else:
                    gfar_ref[s - 1, :span, cut], gfar_ref[s - 1, span:, cut] = gk, gv


def attend_back(numbers, order, own, far, grads, att_t, logs):
    pieces, sides = len(own), 1 + len(far) // len(own)
    span, piece = own[0].shape[0] // 3, own[0].shape[1]
    rows = pieces * piece
    blocks = rows // BLK
    keys = rows * sides
    column = pl.BlockSpec((span, BLK), lambda i, *_: (0, i))
    return pl.pallas_call(
        partial(attend_back_kernel, pieces, sides),
        grid_spec=pltpu.PrefetchScalarGridSpec(
            num_scalar_prefetch=2,
            grid=(blocks,),
            in_specs=[
                pl.BlockSpec((1, span, BLK), lambda i, n, o: (o[i // 2], 0, i % 2)),
                column,
                pl.BlockSpec((1, 8, BLK), lambda i, *_: (i, 0, 0)),
            ]
            + [whole(a.shape) for a in own + far],
            out_specs=[column, whole((2 * span, rows)), whole((sides - 1, 2 * span, rows))],
            scratch_shapes=[
                pltpu.VMEM((span, BLK), f32),
                pltpu.VMEM((span, keys), f32),
                pltpu.VMEM((span, keys), f32),
                pltpu.VMEM((span, rows), bf16),
                pltpu.VMEM((keys, span), bf16),
                pltpu.VMEM((keys, span), bf16),
                pltpu.VMEM((span, keys), bf16),
            ],
        ),
        out_shape=[
            jax.ShapeDtypeStruct((span, rows), bf16),
            jax.ShapeDtypeStruct((2 * span, rows), bf16),
            jax.ShapeDtypeStruct((sides - 1, 2 * span, rows), bf16),
        ],
        compiler_params=PARAMS,
        cost_estimate=cost(30 * rows * keys * span, 16 * keys * span, rows * keys * span // 128),
        name="attend_back",
    )(numbers, order, grads, att_t, logs, *own, *far)


def middle_kernel(att_ref, x_ref, w_ref, vec_ref, slot_ref, mid_ref, normed_ref, send_ref):
    middle = x_ref[...].astype(f32) + dot(att_ref[...], w_ref[...], TN)
    normal, _ = norm_stats(middle)
    normed = (normal * vec_ref[2:3] + vec_ref[3:4]).astype(bf16)
    mid_ref[...] = middle
    normed_ref[...] = normed
    slots = lax.broadcasted_iota(jnp.int32, (send_ref.shape[0], x_ref.shape[0]), 0)
    place = (slots == slot_ref[...]).astype(f32).astype(bf16)
    send_ref[...] = dot(place, normed).astype(bf16)


def middle_step(att_t, rows, weight, vecs, slot, all_slots):
    count, width = rows.shape
    return pl.pallas_call(
        middle_kernel,
        out_shape=[
            jax.ShapeDtypeStruct((count, width), f32),
            jax.ShapeDtypeStruct((count, width), bf16),
            jax.ShapeDtypeStruct((all_slots, width), bf16),
        ],
        compiler_params=PARAMS,
        cost_estimate=cost(2 * count * width * (width + all_slots), 10 * count * width),
        name="middle",
    )(att_t, rows, weight, vecs, slot[None, :])


def turn_kernel(
    got_ref, far_ref, slot_ref, mid_ref, cot_ref, w_ref, vec_ref, gmid_ref, gbr_ref, gatt_ref, sum_ref
):
    slots = lax.broadcasted_iota(jnp.int32, (mid_ref.shape[0], got_ref.shape[0]), 1)
    place = (slots == slot_ref[...]).astype(f32).astype(bf16)
    grad = (dot(place, got_ref[...]) + far_ref[...].astype(f32)).astype(bf16).astype(f32)
    normal, scale = norm_stats(mid_ref[...])
    middle = cot_ref[...].astype(f32) + norm_back(normal, scale, vec_ref[2:3], grad)
    branch = middle.astype(bf16)
    gmid_ref[...] = middle
    gbr_ref[...] = branch
    gatt_ref[...] = dot(w_ref[...], branch, NT).astype(bf16)
    sum_ref[...] = jnp.zeros_like(sum_ref)
    sum_ref[0:1] = jnp.sum(grad * normal, axis=0, keepdims=True)
    sum_ref[1:2] = jnp.sum(grad, axis=0, keepdims=True)


def turn_step(got, far, slot, middle, cot, weight, vecs):
    count, width = middle.shape
    return pl.pallas_call(
        turn_kernel,
        out_shape=[
            jax.ShapeDtypeStruct((count, width), f32),
            jax.ShapeDtypeStruct((count, width), bf16),
            jax.ShapeDtypeStruct((weight.shape[0], count), bf16),
            jax.ShapeDtypeStruct((128, width), f32),
        ],
        compiler_params=PARAMS,
        cost_estimate=cost(2 * count * width * (width + got.shape[0]), 12 * count * width),
        name="turn",
    )(got, far, slot[:, None], middle, cot, weight, vecs)


def out_grad_kernel(att_ref, gbr_ref, sum_ref, out_ref):
    width = gbr_ref.shape[1]
    out_ref[:, :width] = dot(att_ref[...], gbr_ref[...]).astype(bf16)
    out_ref[:, width:] = jnp.transpose(sum_ref[...]).astype(bf16)


def out_grad_step(att_t, gbr, sums):
    return pl.pallas_call(
        out_grad_kernel,
        out_shape=jax.ShapeDtypeStruct((att_t.shape[0], gbr.shape[1] + 128), bf16),
        compiler_params=PARAMS,
        cost_estimate=cost(2 * att_t.size * gbr.shape[1], 6 * gbr.size),
        name="out_grad",
    )(att_t, gbr, sums)


def rows_kernel(gq_ref, gown_ref, got_ref, wt_ref, rows_ref, cols_ref):
    gkv = gown_ref[...].astype(f32)
    for k in range(got_ref.shape[0]):
        gkv = gkv + got_ref[k].astype(f32)
    columns = jnp.concatenate([gq_ref[...], gkv.astype(bf16)], axis=0)
    cols_ref[...] = columns
    rows_ref[0] = dot(columns, wt_ref[...], TN).astype(bf16)


def rows_step(gq, gown, got, wt, rows):
    sources = gq.shape[1] // rows
    wide, width = wt.shape
    return pl.pallas_call(
        rows_kernel,
        grid=(sources,),
        in_specs=[
            pl.BlockSpec((gq.shape[0], rows), lambda i: (0, i)),
            pl.BlockSpec((gown.shape[0], rows), lambda i: (0, i)),
            pl.BlockSpec((got.shape[0], gown.shape[0], rows), lambda i: (0, 0, i)),
            whole(wt.shape),
        ],
        out_specs=[
            pl.BlockSpec((1, rows, width), lambda i: (i, 0, 0)),
            pl.BlockSpec((wide, rows), lambda i: (0, i)),
        ],
        out_shape=[
            jax.ShapeDtypeStruct((sources, rows, width), bf16),
            jax.ShapeDtypeStruct((wide, sources * rows), bf16),
        ],
        compiler_params=PARAMS,
        cost_estimate=cost(2 * sources * rows * width * wide, 4 * sources * rows * width),
        name="rows",
    )(gq, gown, got, wt)


def weights_kernel(cols_ref, rows_ref, vec_ref, *refs):
    sources = rows_ref.shape[0]
    hidden_refs, mixed_ref = refs[:sources], refs[sources]
    piece = rows_ref.shape[1]
    total, gains, biases = None, 0.0, 0.0
    for j, ref in enumerate(hidden_refs):
        normal, _ = norm_stats(ref[...].astype(f32))
        normed = (normal * vec_ref[0:1] + vec_ref[1:2]).astype(bf16)
        rows = rows_ref[j].astype(f32)
        gains += jnp.sum(rows * normal, axis=0, keepdims=True)
        biases += jnp.sum(rows, axis=0, keepdims=True)
        part = dot(cols_ref[:, j * piece : (j + 1) * piece], normed)
        total = part if total is None else total + part
    cores, planes, count, _ = mixed_ref.shape
    wide = total.shape[0]
    weights = jnp.transpose(total).astype(bf16)
    zeros = jnp.zeros((126, total.shape[1]), f32)
    sums = jnp.transpose(jnp.concatenate([gains, biases, zeros], axis=0)).astype(bf16)
    for z in range(planes):
        for s in range(cores):
            at = (z * cores + s) * count
            mixed_ref[s, z, :, :wide] = weights[at : at + count]
            mixed_ref[s, z, :, wide:] = sums[at : at + count]


def weights_step(cols, rows, vecs, hidden, cores, planes):
    wide, width = cols.shape[0], rows.shape[2]
    shape = (cores, planes, width // (cores * planes), wide + 128)
    return pl.pallas_call(
        weights_kernel,
        out_shape=jax.ShapeDtypeStruct(shape, bf16),
        compiler_params=PARAMS,
        cost_estimate=cost(2 * cols.size * width, 4 * rows.size),
        name="weights",
    )(cols, rows, vecs, *hidden)


def assemble_kernel(span, groups, part_ref, out_ref, sum_ref):
    count, rows, _ = part_ref.shape
    cores = count // groups
    for s in range(cores):
        at = slice(s * rows, (s + 1) * rows)
        pieces = [part_ref[g * cores + s].astype(f32) for g in range(groups)]
        out_ref[at, :] = jnp.concatenate(
            [p[:, t * span : (t + 1) * span] for t in range(3) for p in pieces], axis=1
        )
        sum_ref[at, :] = sum(p[:, 3 * span :] for p in pieces)


def assemble(part, span, groups):
    count, rows, wide = part.shape
    total = rows * (count // groups)
    return pl.pallas_call(
        partial(assemble_kernel, span, groups),
        out_shape=[
            jax.ShapeDtypeStruct((total, 3 * span * groups), f32),
            jax.ShapeDtypeStruct((total, wide - 3 * span), f32),
        ],
        compiler_params=PARAMS,
        cost_estimate=cost(part.size, 6 * part.size),
        name="assemble",
    )(part)


def expert_kernel(x_ref, gy_ref, first_ref, second_ref, act_ref, gpre_ref, gn_ref, ey_ref):
    flat = lambda ref: ref[...].reshape(-1, ref.shape[-1])
    first, second = first_ref[0], second_ref[0]
    pre = dot(flat(x_ref), first)
    inner = 0.7978845608028654 * (pre + 0.044715 * (pre * pre * pre))
    bend = jnp.tanh(inner)
    half = 0.5 * (1.0 + bend)
    act = (pre * half).astype(bf16)
    slope = half + 0.5 * pre * (1.0 - bend * bend) * (
        0.7978845608028654 * (1.0 + 3 * 0.044715 * (pre * pre))
    )
    gpre = (dot(flat(gy_ref), second) * slope).astype(bf16)
    act_ref[...] = act.reshape(act_ref.shape)
    gpre_ref[...] = gpre.reshape(gpre_ref.shape)
    gn_ref[...] = dot(gpre, first, NT).astype(bf16).reshape(gn_ref.shape)
    ey_ref[...] = dot(act, second, NT).astype(bf16).reshape(ey_ref.shape)


def expert_step(tokens, grads, first, second):
    sources, experts, room, width = tokens.shape
    hidden = first.shape[2]
    token_spec = pl.BlockSpec((sources, 1, room, width), lambda e: (0, e, 0, 0))
    hidden_spec = pl.BlockSpec((sources, 1, room, hidden), lambda e: (0, e, 0, 0))
    weight_spec = pl.BlockSpec((1, width, hidden), lambda e: (e, 0, 0))
    like = lambda last: jax.ShapeDtypeStruct((sources, experts, room, last), bf16)
    return pl.pallas_call(
        expert_kernel,
        grid=(experts,),
        in_specs=[token_spec, token_spec, weight_spec, weight_spec],
        out_specs=[hidden_spec, hidden_spec, token_spec, token_spec],
        out_shape=[like(hidden), like(hidden), like(width), like(width)],
        compiler_params=PARAMS,
        cost_estimate=pl.CostEstimate(
            flops=8 * sources * experts * room * width * hidden,
            bytes_accessed=4 * first.size + 12 * tokens.size,
            transcendentals=sources * experts * room * hidden,
        ),
        name="expert_step",
    )(tokens, grads, first, second)


def expert_grad_kernel(parts, *refs):
    flat = lambda ref: ref[...].reshape(-1, ref.shape[-1])
    stack = lambda some: jnp.concatenate([flat(r) for r in some], axis=0)
    ins, (gfirst_ref, gsecond_ref) = refs[: 4 * parts], refs[4 * parts :]
    tokens, grads, acts, gpres = (stack(ins[i * parts : (i + 1) * parts]) for i in range(4))
    gfirst_ref[0] = dot(tokens, gpres, TN)
    gsecond_ref[0] = dot(grads, acts, TN)


def expert_grads(tokens, grads, acts, gpres):
    parts = len(tokens)
    sources, experts, room, width = tokens[0].shape
    hidden = acts[0].shape[3]
    spec = lambda last: pl.BlockSpec((sources, 1, room, last), lambda e: (0, e, 0, 0))
    out_spec = pl.BlockSpec((1, width, hidden), lambda e: (e, 0, 0))
    out = jax.ShapeDtypeStruct((experts, width, hidden), f32)
    return pl.pallas_call(
        partial(expert_grad_kernel, parts),
        grid=(experts,),
        in_specs=[spec(width)] * (2 * parts) + [spec(hidden)] * (2 * parts),
        out_specs=[out_spec, out_spec],
        out_shape=[out, out],
        compiler_params=PARAMS,
        cost_estimate=pl.CostEstimate(
            flops=4 * parts * sources * experts * room * width * hidden,
            bytes_accessed=8 * experts * width * hidden,
            transcendentals=0,
        ),
        name="expert_grads",
    )(*tokens, *grads, *acts, *gpres)


def local(
    hidden_in, token_ids, hash_table, deal_order, qkv_weight, out_weight,
    norm1_gain, norm1_bias, norm2_gain, norm2_bias, expert_in, expert_out, out_grad,
):
    devices = lax.axis_size("ctx")
    position = lax.axis_index("ctx")
    planes = lax.axis_size("fsdp")
    plane = lax.axis_index("fsdp")
    width = hidden_in.shape[2]
    local_experts = expert_in.shape[0]
    experts = local_experts * devices
    room = 2 * TOK_DEV // experts
    all_slots = experts * room
    groups = gcd(HEADS, devices)
    cores = devices // groups
    group, core = position // cores, position % cores
    span = width // groups
    across = [[g * cores + c for g in range(groups)] for c in range(cores)]

    own_hidden = hidden_in[0]
    out_cot = out_grad[0]

    expert_of = hash_table[token_ids[0]]
    same = expert_of[:, None] == expert_of[None, :]
    shape = (TOK_DEV, TOK_DEV)
    before = lax.broadcasted_iota(jnp.int32, shape, 1) < lax.broadcasted_iota(jnp.int32, shape, 0)
    slot = expert_of * room + jnp.sum((same & before).astype(jnp.int32), axis=1)

    def spread(value):
        far = [None, None]
        for k in range(2, planes):
            far.append(swap(far[k - 1], "fsdp", 1) if k % 2 else swap(value, "fsdp", k))
        return far

    counter = lambda axis: lax.broadcasted_iota(
        jnp.int32, (all_slots, TOK_DEV) if axis == 0 else (TOK_DEV, all_slots), axis
    )
    place = lambda s, rows: dot((counter(0) == s[None, :]).astype(bf16), rows).astype(bf16)
    fetch = lambda s, rows: dot((counter(1) == s[:, None]).astype(bf16), rows)
    packed = (devices, local_experts * room, width)
    shaped = (devices, local_experts, room, width)
    exchange = lambda rows: trade(rows.reshape(packed), "ctx").reshape(shaped)
    evens = range(2, planes, 2)

    cut = lambda part: lax.dynamic_slice_in_dim(qkv_weight, part * width + group * span, span, 1)
    vecs = jnp.stack([norm1_gain, norm1_bias, norm2_gain, norm2_bias], axis=1)
    own_cols = jnp.concatenate(
        [cut(0), cut(1), cut(2), jnp.pad(vecs, ((0, 0), (0, 60)))], axis=1
    )
    full = lax.all_gather(own_cols, "fsdp", axis=0, tiled=True)
    wt, vecs = full[:, : 3 * span].T, full[:, 3 * span : 3 * span + 4].T.astype(f32)
    hidden = [own_hidden] + [swap(own_hidden, "ctx", j * cores) for j in range(1, groups)]
    far_cots = {k: swap(out_cot, "fsdp", k) for k in evens}
    far_slots = spread(slot)

    near_first = [place(slot, out_cot)] + [place(far_slots[k], far_cots[k]) for k in evens]
    sides = len(near_first)
    stacked = after(jnp.stack([p.reshape(packed) for p in near_first], axis=1), *hidden)
    got_near = trade(stacked, "ctx")
    got_far = swap(got_near, "fsdp", 1)
    gys = [None] * planes
    for i, k in enumerate([0, *evens]):
        gys[k] = got_near[:, i].reshape(shaped)
        gys[k + 1] = got_far[:, i].reshape(shaped)

    own = [project(h, wt, vecs) for h in hidden]
    far = [swap(o[span:], "ctx", k) for k in range(1, cores) for o in own]
    out_full = lax.all_gather(out_weight, "fsdp", axis=0, tiled=True)
    table = deal_order.reshape(groups, cores)
    order = group ^ jnp.arange(groups, dtype=jnp.int32)
    low = jnp.stack(
        [lax.dynamic_index_in_dim(table, core ^ s, 1, False)[order] for s in range(cores)]
    )
    numbers = jnp.stack([low, 2 * devices - 1 - low], axis=2).reshape(-1)
    att, att_f, logs = attend(numbers, order, own, far)
    att = after(att, got_near)
    att_t = trade(att, "ctx", across).reshape(width, TOK_DEV)
    middle, normed, sent = middle_step(att_t, own_hidden, out_full, vecs, slot, all_slots)

    tokens = [exchange(sent)]
    tokens.append(swap(tokens[0], "fsdp", 1))
    for k in evens:
        rows = swap(normed, "fsdp", k)
        send = place(far_slots[k], after(rows, got_far))
        tokens.append(exchange(send))
        rows = swap(after(rows, send), "fsdp", 1)
        tokens.append(exchange(place(far_slots[k + 1], rows)))
    acts, gpres, gns, eys = [], [], [], []
    for k in range(planes):
        act, gpre, gn, ey = expert_step(tokens[k], gys[k], expert_in, expert_out)
        acts.append(act)
        gpres.append(gpre)
        gns.append(gn)
        eys.append(ey)
    grad_expert_in, grad_expert_out = expert_grads(tokens, gys, acts, gpres)

    far_grad = jnp.zeros((TOK_DEV, width), f32)
    for k in evens:
        last = fetch(far_slots[k + 1], exchange(gns[k + 1]).reshape(all_slots, width)).astype(bf16)
        back = fetch(far_slots[k], exchange(gns[k]).reshape(all_slots, width))
        back = (back + swap(last, "fsdp", 1).astype(f32)).astype(bf16)
        far_grad = far_grad + swap(back, "fsdp", k).astype(f32)
    near = (gns[0].astype(f32) + swap(gns[1], "fsdp", 1).astype(f32)).astype(bf16)
    near = exchange(near).reshape(all_slots, width)
    far_grad = after(far_grad.astype(bf16), near, grad_expert_in)
    grad_middle, branch, gatt, sums_two = turn_step(
        near, far_grad, slot, middle, out_cot, out_full, vecs
    )
    gatt = trade(gatt.reshape(groups, span, TOK_DEV), "ctx", across)
    outs = out_grad_step(att_t, branch, sums_two)

    total_y = eys[0].astype(f32) + swap(eys[1], "fsdp", 1).astype(f32)
    for k in evens:
        back = (eys[k].astype(f32) + swap(eys[k + 1], "fsdp", 1).astype(f32)).astype(bf16)
        total_y = total_y + swap(back, "fsdp", k).astype(f32)
    token_y = fetch(slot, exchange(total_y.astype(bf16)).reshape(all_slots, width))
    layer_out = (middle + token_y).astype(bf16)

    gq, gown, gfar = attend_back(numbers, order, own, far, gatt, att_f, logs)
    got = jnp.stack([swap(gfar[k - 1], "ctx", k) for k in range(1, cores)])
    grad_rows, grad_cols = rows_step(gq, gown, got, wt, TOK_DEV)
    grad_normed = grad_rows[0].astype(f32)
    for j in range(1, groups):
        grad_normed = grad_normed + swap(grad_rows[j], "ctx", j * cores).astype(f32)
    mixed = weights_step(grad_cols, grad_rows, vecs, hidden, cores, planes)
    own_normal, own_scale = norm_stats(own_hidden.astype(f32))
    grad_hidden = grad_middle + norm_back(own_normal, own_scale, vecs[0], grad_normed)

    def keep(parts, index, axis, stride):
        pick = lambda k: lax.dynamic_index_in_dim(parts, index ^ k, 0, False)
        total = pick(0).astype(f32)
        for k in range(1, parts.shape[0]):
            total = total + swap(pick(k), axis, k * stride).astype(f32)
        return total.astype(bf16)

    part = keep(keep(mixed, core, "ctx", 1), plane, "fsdp", 1)
    grad_qkv, vec_one = assemble(share(part, devices, "ctx"), span, groups)

    rows = width // planes
    wide = outs.shape[1]
    part = jnp.moveaxis(outs.reshape(planes, devices, rows // devices, wide), 1, 0)
    part = jnp.sum(trade(part, "ctx").astype(f32), axis=0).astype(bf16)
    part = keep(part, plane, "fsdp", 1)
    part = share(part, devices, "ctx").reshape(rows, wide).astype(f32)
    return (
        layer_out[None],
        grad_hidden[None],
        grad_qkv,
        part[:, :width],
        vec_one[:, 0],
        vec_one[:, 1],
        part[:, width],
        part[:, width + 1],
        grad_expert_in,
        grad_expert_out,
    )


def solution(mesh):
    return jax.shard_map(
        local,
        mesh=mesh,
        in_specs=(
            P("fsdp", "ctx", None),
            P("fsdp", "ctx"),
            P(),
            P(),
            P("fsdp", None),
            P("fsdp", None),
            P("fsdp"),
            P("fsdp"),
            P("fsdp"),
            P("fsdp"),
            P("ctx", None, "fsdp"),
            P("ctx", None, "fsdp"),
            P("fsdp", "ctx", None),
        ),
        out_specs=(
            P("fsdp", "ctx", None),
            P("fsdp", "ctx", None),
            P("fsdp", None),
            P("fsdp", None),
            P("fsdp"),
            P("fsdp"),
            P("fsdp"),
            P("fsdp"),
            P("ctx", None, "fsdp"),
            P("ctx", None, "fsdp"),
        ),
        check_vma=False,
    )
```

```python
from functools import partial
from math import gcd

import jax
import jax.numpy as jnp
from jax import lax
from jax.experimental import pallas as pl
from jax.experimental.pallas import tpu as pltpu
from jax.sharding import PartitionSpec as P

HEADS = 12
HD = 64
BLK = 256
TOK_DEV = 512
CHUNK = 4
COST = 1000
epsilon = 1e-05
masked_value = -1e30
bf16 = jnp.bfloat16
f32 = jnp.float32
NT = (((1,), (1,)), ((), ()))
NN = (((1,), (0,)), ((), ()))
TN = (((0,), (0,)), ((), ()))
PARAMS = pltpu.CompilerParams(vmem_limit_bytes=56 * 1024 * 1024)


def dot(a, b, dims=NN):
    return lax.dot_general(a, b, dims, preferred_element_type=f32)


def swap(value, axis, offset):
    size = lax.axis_size(axis)
    return lax.ppermute(value, axis, [(i, i ^ offset) for i in range(size)])


def plain_trade(parts, axis, groups=None):
    return lax.all_to_all(parts, axis, 0, 0, tiled=True, axis_index_groups=groups)


def share(part, count, axis, groups, trade):
    return trade(jnp.broadcast_to(part[None], (count,) + part.shape), axis, groups)


def in_order(pieces, index):
    count, bit = len(pieces), 1
    while bit < count:
        odd = (index & bit) != 0
        pieces = [jnp.where(odd, pieces[i ^ bit], pieces[i]) for i in range(count)]
        bit *= 2
    return pieces


def after(value, *others):
    return lax.optimization_barrier((value,) + others)[0]


def norm_stats(values):
    center = jnp.mean(values, axis=-1, keepdims=True)
    offset = values - center
    scale = lax.rsqrt(jnp.mean(offset * offset, axis=-1, keepdims=True) + epsilon)
    return offset * scale, scale


def norm_back(normal, scale, gain, grad):
    inner = grad * gain
    return scale * (
        inner
        - jnp.mean(inner, axis=-1, keepdims=True)
        - normal * jnp.mean(inner * normal, axis=-1, keepdims=True)
    )


def whole(shape):
    return pl.BlockSpec(shape, lambda i, *_: (0,) * len(shape), pipeline_mode=pl.Buffered(1))


def cost(flops, moved, exps=0):
    return pl.CostEstimate(flops=int(flops) // COST, bytes_accessed=int(moved) // COST, transcendentals=int(exps) // COST)


def project_kernel(pieces, *refs):
    wt_ref, vec_ref, q_ref, kv_ref = refs[pieces:]
    span, rows = q_ref.shape[0], refs[0].shape[0]
    for p, ref in enumerate(refs[:pieces]):
        normal, _ = norm_stats(ref[...].astype(f32))
        normed = (normal * vec_ref[0:1] + vec_ref[1:2]).astype(bf16)
        got = dot(wt_ref[...], normed, NT).astype(bf16)
        cut = slice(p * rows, (p + 1) * rows)
        q_ref[:, cut] = (got[:span].astype(f32) * HD ** (-0.5)).astype(bf16)
        kv_ref[:, cut] = got[span:]


def project(hidden, wt, vecs):
    rows, width = hidden[0].shape
    span = wt.shape[0] // 3
    total = len(hidden) * rows
    return pl.pallas_call(
        partial(project_kernel, len(hidden)),
        out_shape=[
            jax.ShapeDtypeStruct((span, total), bf16),
            jax.ShapeDtypeStruct((2 * span, total), bf16),
        ],
        compiler_params=PARAMS,
        cost_estimate=cost(6 * total * width * span, 4 * total * width),
        name="project",
    )(*hidden, wt, vecs)


def only_head(block, head):
    heads = block.shape[0] // HD
    zero = jnp.zeros((HD, block.shape[1]), block.dtype)
    return jnp.concatenate(
        [block[h * HD : (h + 1) * HD] if h == head else zero for h in range(heads)], axis=0
    )


def key_blocks(number_ref, kv_refs, high=1):
    place = 0
    for ref in kv_refs:
        for i in range(ref.shape[1] // BLK):
            if high or i % 2 == 0:
                at = pl.multiple_of(number_ref[place] * BLK, BLK)
                yield at, ref[:, i * BLK : (i + 1) * BLK]
            place += 1


def take_queries(q_refs, q_all):
    at = 0
    for ref in q_refs:
        q_all[:, at : at + ref.shape[1]] = ref[...]
        at += ref.shape[1]


def attend_kernel(high, parts, all_parts, number_ref, order_ref, *refs):
    q_refs, kv_refs = refs[:parts], refs[parts:all_parts]
    att_ref, att_t_ref, lse_ref, acc_ref, q_all, k_sorted, v_sorted = refs[-7:]
    turn = pl.program_id(0)
    span = acc_ref.shape[0]
    heads = span // HD
    block = number_ref[2 * turn + high]
    size = CHUNK * BLK

    @pl.when(turn == 0)
    def _():
        take_queries(q_refs, q_all)
        for at, kv in key_blocks(number_ref, kv_refs, high):
            k_sorted[pl.ds(at, BLK), :] = jnp.transpose(kv[:span])
            v_sorted[:, pl.ds(at, BLK)] = kv[span:]

    own_queries = q_all[:, pl.ds(pl.multiple_of((2 * turn + high) * BLK, BLK), BLK)]
    queries = [only_head(own_queries, h) for h in range(heads)]
    acc_ref[...] = jnp.zeros_like(acc_ref)

    def step(last, index, state):
        top, total = state
        at = pl.multiple_of(index * size, size)
        keys = k_sorted[pl.ds(at, size), :]
        tops, totals = [], []
        scores = [dot(keys, queries[h]) for h in range(heads)]
        if last:
            row = lax.broadcasted_iota(jnp.int32, scores[0].shape, 0)
            limit = (block + 1 - index * CHUNK) * BLK
            scores = [jnp.where(row < limit, s, masked_value) for s in scores]
        for h in range(heads):
            rows = slice(h * HD, (h + 1) * HD)
            new_top = jnp.maximum(top[h], jnp.max(scores[h], axis=0, keepdims=True))
            factor = jnp.exp(top[h] - new_top)
            weights = jnp.exp(scores[h] - new_top)
            tops.append(new_top)
            totals.append(total[h] * factor + jnp.sum(weights, axis=0, keepdims=True))
            update = dot(v_sorted[rows, pl.ds(at, size)], weights.astype(bf16))
            acc_ref[rows, :] = acc_ref[rows, :] * factor + update
        return tuple(tops), tuple(totals)

    start = (
        tuple(jnp.full((1, BLK), masked_value, f32) for _ in range(heads)),
        tuple(jnp.zeros((1, BLK), f32) for _ in range(heads)),
    )
    full = (block + 1) // CHUNK
    state = lax.fori_loop(0, full, partial(step, False), start)
    top, total = lax.fori_loop(full, (block + CHUNK) // CHUNK, partial(step, True), state)
    for h in range(heads):
        rows = slice(h * HD, (h + 1) * HD)
        out = acc_ref[rows, :] / total[h]
        att_t_ref[rows, :] = out
        att_ref[0, rows, :] = out.astype(bf16)
        lse_ref[0, h : h + 1, :] = top[h] + jnp.log(total[h])


def attend(numbers, order, queries, kvs, before):
    high = 0 if before is None else 1
    before = () if before is None else tuple(before)
    pieces, span = order.shape[0], queries[0].shape[0]
    rows, keys = sum(q.shape[1] for q in queries), sum(kv.shape[1] for kv in kvs)
    piece, blocks = rows // pieces, rows // BLK
    sorted_keys = keys if high else keys // 2
    return pl.pallas_call(
        partial(attend_kernel, high, len(queries), len(queries + kvs)),
        grid_spec=pltpu.PrefetchScalarGridSpec(
            num_scalar_prefetch=2,
            grid=(blocks // 2,),
            in_specs=[whole(a.shape) for a in queries + kvs]
            + [pl.BlockSpec(memory_space=pl.ANY)] * len(before),
            out_specs=[
                pl.BlockSpec((1, span, BLK), lambda i, n, o: (o[i], 0, high)),
                pl.BlockSpec((span, BLK), lambda i, *_: (0, 2 * i + high)),
                pl.BlockSpec((1, 8, BLK), lambda i, *_: (2 * i + high, 0, 0)),
            ],
            scratch_shapes=[
                pltpu.VMEM((span, BLK), f32),
                pltpu.VMEM((span, rows), bf16),
                pltpu.VMEM((sorted_keys, span), bf16),
                pltpu.VMEM((span, sorted_keys), bf16),
            ],
        ),
        out_shape=[
            jax.ShapeDtypeStruct((pieces, span, piece), bf16),
            jax.ShapeDtypeStruct((span, rows), f32),
            jax.ShapeDtypeStruct((blocks, 8, BLK), f32),
        ],
        compiler_params=PARAMS,
        cost_estimate=cost(12 * rows * keys * span, 8 * keys * span, rows * keys * span // 128),
        input_output_aliases={2 + len(queries + kvs) + i: i for i in range(len(before))},
        name="attend_high" if high else "attend_low",
    )(numbers, order, *queries, *kvs, *before)


def attend_back_kernel(parts, all_parts, number_ref, order_ref, g_ref, att_t_ref, lse_ref, *refs):
    q_refs, kv_refs = refs[:parts], refs[parts:all_parts]
    gq_ref, gown_ref, gfar_ref = refs[all_parts : all_parts + 3]
    gq_acc, gk_acc, gv_acc, q_all, k_sorted, v_sorted, kt_sorted = refs[all_parts + 3 :]
    sides = 1 + gfar_ref.shape[0]
    turn = pl.program_id(0)
    span = gq_acc.shape[0]
    heads = span // HD
    block = number_ref[turn]
    size = CHUNK * BLK

    @pl.when(turn == 0)
    def _():
        gk_acc[...] = jnp.zeros_like(gk_acc)
        gv_acc[...] = jnp.zeros_like(gv_acc)
        take_queries(q_refs, q_all)
        for at, kv in key_blocks(number_ref, kv_refs):
            k_sorted[pl.ds(at, BLK), :] = jnp.transpose(kv[:span])
            v_sorted[pl.ds(at, BLK), :] = jnp.transpose(kv[span:])
            kt_sorted[:, pl.ds(at, BLK)] = kv[:span]

    grads = g_ref[0]
    queries = q_all[:, pl.ds(pl.multiple_of(turn * BLK, BLK), BLK)]
    prod = grads.astype(f32) * att_t_ref[...]
    part = lambda h: slice(h * HD, (h + 1) * HD)
    deltas = [jnp.sum(prod[part(h)], axis=0, keepdims=True) for h in range(heads)]
    logs = [lse_ref[0, h : h + 1, :] for h in range(heads)]
    q_only = [only_head(queries, h) for h in range(heads)]
    g_only = [only_head(grads, h) for h in range(heads)]
    gq_acc[...] = jnp.zeros_like(gq_acc)

    def step(last, index, carry):
        at = pl.multiple_of(index * size, size)
        keys = k_sorted[pl.ds(at, size), :]
        values = v_sorted[pl.ds(at, size), :]
        if last:
            row = lax.broadcasted_iota(jnp.int32, (size, BLK), 0)
            allowed = row < (block + 1 - index * CHUNK) * BLK
        for h in range(heads):
            rows = part(h)
            probs = jnp.exp(dot(keys, q_only[h]) - logs[h])
            if last:
                probs = jnp.where(allowed, probs, 0.0)
            gs = (probs * (dot(values, g_only[h]) - deltas[h])).astype(bf16)
            gq_acc[rows, :] += dot(kt_sorted[rows, pl.ds(at, size)], gs)
            gv_acc[rows, pl.ds(at, size)] += dot(grads[rows], probs.astype(bf16), NT)
            gk_acc[rows, pl.ds(at, size)] += dot(queries[rows], gs, NT)
        return carry

    full = (block + 1) // CHUNK
    lax.fori_loop(0, full, partial(step, False), 0)
    lax.fori_loop(full, (block + CHUNK) // CHUNK, partial(step, True), 0)
    gq_ref[...] = (gq_acc[...] * HD ** (-0.5)).astype(bf16)

    @pl.when(turn == pl.num_programs(0) - 1)
    def _():
        per = gown_ref.shape[1] // BLK
        for s in range(sides):
            for i in range(per):
                at = pl.multiple_of(number_ref[s * per + i] * BLK, BLK)
                cut = slice(i * BLK, (i + 1) * BLK)
                gk = gk_acc[:, pl.ds(at, BLK)].astype(bf16)
                gv = gv_acc[:, pl.ds(at, BLK)].astype(bf16)
                if s == 0:
                    gown_ref[:span, cut], gown_ref[span:, cut] = gk, gv
                else:
                    gfar_ref[s - 1, :span, cut], gfar_ref[s - 1, span:, cut] = gk, gv


def attend_back(numbers, order, queries, kvs, grads, att_t, logs):
    span = queries[0].shape[0]
    rows, keys = sum(q.shape[1] for q in queries), sum(kv.shape[1] for kv in kvs)
    sides, blocks = keys // rows, rows // BLK
    column = pl.BlockSpec((span, BLK), lambda i, *_: (0, i))
    return pl.pallas_call(
        partial(attend_back_kernel, len(queries), len(queries + kvs)),
        grid_spec=pltpu.PrefetchScalarGridSpec(
            num_scalar_prefetch=2,
            grid=(blocks,),
            in_specs=[
                pl.BlockSpec((1, span, BLK), lambda i, n, o: (o[i // 2], 0, i % 2)),
                column,
                pl.BlockSpec((1, 8, BLK), lambda i, *_: (i, 0, 0)),
            ]
            + [whole(a.shape) for a in queries + kvs],
            out_specs=[column, whole((2 * span, rows)), whole((sides - 1, 2 * span, rows))],
            scratch_shapes=[
                pltpu.VMEM((span, BLK), f32),
                pltpu.VMEM((span, keys), f32),
                pltpu.VMEM((span, keys), f32),
                pltpu.VMEM((span, rows), bf16),
                pltpu.VMEM((keys, span), bf16),
                pltpu.VMEM((keys, span), bf16),
                pltpu.VMEM((span, keys), bf16),
            ],
        ),
        out_shape=[
            jax.ShapeDtypeStruct((span, rows), bf16),
            jax.ShapeDtypeStruct((2 * span, rows), bf16),
            jax.ShapeDtypeStruct((sides - 1, 2 * span, rows), bf16),
        ],
        compiler_params=PARAMS,
        cost_estimate=cost(30 * rows * keys * span, 16 * keys * span, rows * keys * span // 128),
        name="attend_back",
    )(numbers, order, grads, att_t, logs, *queries, *kvs)


def middle_kernel(att_ref, x_ref, w_ref, vec_ref, slot_ref, mid_ref, normed_ref, send_ref):
    middle = x_ref[...].astype(f32) + dot(att_ref[...], w_ref[...], TN)
    normal, _ = norm_stats(middle)
    normed = (normal * vec_ref[2:3] + vec_ref[3:4]).astype(bf16)
    mid_ref[...] = middle
    normed_ref[...] = normed
    slots = lax.broadcasted_iota(jnp.int32, (send_ref.shape[0], x_ref.shape[0]), 0)
    place = (slots == slot_ref[...]).astype(f32).astype(bf16)
    send_ref[...] = dot(place, normed).astype(bf16)


def middle_step(att_t, rows, weight, vecs, slot, all_slots):
    count, width = rows.shape
    return pl.pallas_call(
        middle_kernel,
        out_shape=[
            jax.ShapeDtypeStruct((count, width), f32),
            jax.ShapeDtypeStruct((count, width), bf16),
            jax.ShapeDtypeStruct((all_slots, width), bf16),
        ],
        compiler_params=PARAMS,
        cost_estimate=cost(2 * count * width * (width + all_slots), 10 * count * width),
        name="middle",
    )(att_t, rows, weight, vecs, slot[None, :])


def turn_kernel(
    got_ref, far_ref, slot_ref, mid_ref, cot_ref, w_ref, vec_ref, gmid_ref, gbr_ref, gatt_ref, sum_ref
):
    slots = lax.broadcasted_iota(jnp.int32, (mid_ref.shape[0], got_ref.shape[0]), 1)
    place = (slots == slot_ref[...]).astype(f32).astype(bf16)
    grad = (dot(place, got_ref[...]) + far_ref[...].astype(f32)).astype(bf16).astype(f32)
    normal, scale = norm_stats(mid_ref[...])
    middle = cot_ref[...].astype(f32) + norm_back(normal, scale, vec_ref[2:3], grad)
    branch = middle.astype(bf16)
    gmid_ref[...] = middle
    gbr_ref[...] = branch
    gatt_ref[...] = dot(w_ref[...], branch, NT).astype(bf16)
    sum_ref[...] = jnp.zeros_like(sum_ref)
    sum_ref[0:1] = jnp.sum(grad * normal, axis=0, keepdims=True)
    sum_ref[1:2] = jnp.sum(grad, axis=0, keepdims=True)


def turn_step(got, far, slot, middle, cot, weight, vecs):
    count, width = middle.shape
    return pl.pallas_call(
        turn_kernel,
        out_shape=[
            jax.ShapeDtypeStruct((count, width), f32),
            jax.ShapeDtypeStruct((count, width), bf16),
            jax.ShapeDtypeStruct((weight.shape[0], count), bf16),
            jax.ShapeDtypeStruct((128, width), f32),
        ],
        compiler_params=PARAMS,
        cost_estimate=cost(2 * count * width * (width + got.shape[0]), 12 * count * width),
        name="turn",
    )(got, far, slot[:, None], middle, cot, weight, vecs)


def out_grad_kernel(planes, att_ref, gbr_ref, sum_ref, out_ref):
    count = out_ref.shape[0]
    weights = dot(att_ref[...], gbr_ref[...])
    step = weights.shape[0] // (planes * count)
    for c in range(count):
        at = [(z * count + c) * step for z in range(planes)]
        pieces = [weights[a : a + step] for a in at] + [sum_ref[:16]]
        out_ref[c] = jnp.concatenate(pieces, axis=0).astype(bf16)


def out_grad_step(att_t, gbr, sums, planes, devices):
    rows = att_t.shape[0] // devices + 16
    return pl.pallas_call(
        partial(out_grad_kernel, planes),
        out_shape=jax.ShapeDtypeStruct((devices, rows, gbr.shape[1]), bf16),
        compiler_params=PARAMS,
        cost_estimate=cost(2 * att_t.size * gbr.shape[1], 6 * gbr.size),
        name="out_grad",
    )(att_t, gbr, sums)


def rows_kernel(order_ref, gq_ref, gown_ref, got_ref, wt_ref, cols_ref, out_ref):
    rows = out_ref.shape[1]
    for j in range(out_ref.shape[0]):
        cut = slice(j * rows, (j + 1) * rows)
        gkv = gown_ref[:, cut].astype(f32)
        for k in range(got_ref.shape[0]):
            gkv = gkv + got_ref[k, :, cut].astype(f32)
        columns = jnp.concatenate([gq_ref[:, cut], gkv.astype(bf16)], axis=0)
        cols_ref[:, cut] = columns
        out_ref[order_ref[j]] = dot(columns, wt_ref[...], TN).astype(bf16)


SCALARS = pl.BlockSpec(memory_space=pltpu.SMEM)
ARRAY = pl.BlockSpec(memory_space=pltpu.VMEM)


def rows_step(order, gq, gown, got, wt, rows):
    sources = gq.shape[1] // rows
    wide, width = wt.shape
    return pl.pallas_call(
        rows_kernel,
        in_specs=[SCALARS] + [ARRAY] * 4,
        out_shape=[
            jax.ShapeDtypeStruct((wide, sources * rows), bf16),
            jax.ShapeDtypeStruct((sources, rows, width), bf16),
        ],
        compiler_params=PARAMS,
        cost_estimate=cost(2 * sources * rows * width * wide, 4 * sources * rows * width),
        name="rows",
    )(order, gq, gown, got, wt)


def weights_kernel(order_ref, cols_ref, vec_ref, rows_ref, *refs):
    hidden_refs, mixed_ref = refs[:-1], refs[-1]
    piece = rows_ref.shape[1]
    total, gains, biases = None, 0.0, 0.0
    for j, ref in enumerate(hidden_refs):
        normal, _ = norm_stats(ref[...].astype(f32))
        normed = (normal * vec_ref[0:1] + vec_ref[1:2]).astype(bf16)
        rows = rows_ref[order_ref[j]].astype(f32)
        gains += jnp.sum(rows * normal, axis=0, keepdims=True)
        biases += jnp.sum(rows, axis=0, keepdims=True)
        part = dot(cols_ref[:, j * piece : (j + 1) * piece], normed)
        total = part if total is None else total + part
    cores, planes, count, _ = mixed_ref.shape
    wide = total.shape[0]
    weights = jnp.transpose(total).astype(bf16)
    zeros = jnp.zeros((126, total.shape[1]), f32)
    sums = jnp.transpose(jnp.concatenate([gains, biases, zeros], axis=0)).astype(bf16)
    for z in range(planes):
        for s in range(cores):
            at = (z * cores + s) * count
            mixed_ref[s, z, :, :wide] = weights[at : at + count]
            mixed_ref[s, z, :, wide : wide + 128] = sums[at : at + count]
            rest = mixed_ref.shape[3] - wide - 128
            mixed_ref[s, z, :, wide + 128 :] = jnp.zeros((count, rest), bf16)


def weights_step(order, cols, rows, vecs, hidden, cores, planes):
    wide, width = cols.shape[0], rows.shape[2]
    shape = (cores, planes, width // (cores * planes), width)
    return pl.pallas_call(
        weights_kernel,
        in_specs=[SCALARS] + [ARRAY] * (3 + len(hidden)),
        out_shape=jax.ShapeDtypeStruct(shape, bf16),
        compiler_params=PARAMS,
        cost_estimate=cost(2 * cols.size * width, 4 * cols.size),
        name="weights",
    )(order, cols, vecs, rows, *hidden)


def assemble_kernel(span, groups, part_ref, out_ref, sum_ref):
    count, rows = part_ref.shape[0], out_ref.shape[0] // (part_ref.shape[0] // groups)
    cores = count // groups
    for s in range(cores):
        at = slice(s * rows, (s + 1) * rows)
        pieces = [part_ref[g * cores + s, :rows].astype(f32) for g in range(groups)]
        out_ref[at, :] = jnp.concatenate(
            [p[:, t * span : (t + 1) * span] for t in range(3) for p in pieces], axis=1
        )
        sum_ref[at, :] = sum(p[:, 3 * span : 3 * span + 128] for p in pieces)


def assemble(part, rows, span, groups):
    count = part.shape[0]
    total = rows * (count // groups)
    return pl.pallas_call(
        partial(assemble_kernel, span, groups),
        out_shape=[
            jax.ShapeDtypeStruct((total, 3 * span * groups), f32),
            jax.ShapeDtypeStruct((total, 128), f32),
        ],
        compiler_params=PARAMS,
        cost_estimate=cost(part.size, 6 * part.size),
        name="assemble",
    )(part)


def expert_kernel(x_ref, gy_ref, first_ref, second_ref, act_ref, gpre_ref, gn_ref, ey_ref):
    flat = lambda ref: ref[...].reshape(-1, ref.shape[-1])
    first, second = first_ref[0], second_ref[0]
    pre = dot(flat(x_ref), first)
    inner = 0.7978845608028654 * (pre + 0.044715 * (pre * pre * pre))
    bend = jnp.tanh(inner)
    half = 0.5 * (1.0 + bend)
    act = (pre * half).astype(bf16)
    slope = half + 0.5 * pre * (1.0 - bend * bend) * (
        0.7978845608028654 * (1.0 + 3 * 0.044715 * (pre * pre))
    )
    gpre = (dot(flat(gy_ref), second) * slope).astype(bf16)
    act_ref[...] = act.reshape(act_ref.shape)
    gpre_ref[...] = gpre.reshape(gpre_ref.shape)
    gn_ref[...] = dot(gpre, first, NT).astype(bf16).reshape(gn_ref.shape)
    ey_ref[...] = dot(act, second, NT).astype(bf16).reshape(ey_ref.shape)


def expert_step(tokens, grads, first, second):
    sources, experts, room, width = tokens.shape
    hidden = first.shape[2]
    token_spec = pl.BlockSpec((sources, 1, room, width), lambda e: (0, e, 0, 0))
    hidden_spec = pl.BlockSpec((sources, 1, room, hidden), lambda e: (0, e, 0, 0))
    weight_spec = pl.BlockSpec((1, width, hidden), lambda e: (e, 0, 0))
    like = lambda last: jax.ShapeDtypeStruct((sources, experts, room, last), bf16)
    return pl.pallas_call(
        expert_kernel,
        grid=(experts,),
        in_specs=[token_spec, token_spec, weight_spec, weight_spec],
        out_specs=[hidden_spec, hidden_spec, token_spec, token_spec],
        out_shape=[like(hidden), like(hidden), like(width), like(width)],
        compiler_params=PARAMS,
        cost_estimate=cost(8 * sources * experts * room * width * hidden, 4 * first.size + 12 * tokens.size, sources * experts * room * hidden),
        name="expert_step",
    )(tokens, grads, first, second)


def expert_grad_kernel(parts, *refs):
    flat = lambda ref: ref[...].reshape(-1, ref.shape[-1])
    stack = lambda some: jnp.concatenate([flat(r) for r in some], axis=0)
    ins, (gfirst_ref, gsecond_ref) = refs[: 4 * parts], refs[4 * parts :]
    tokens, grads, acts, gpres = (stack(ins[i * parts : (i + 1) * parts]) for i in range(4))
    gfirst_ref[0] = dot(tokens, gpres, TN)
    gsecond_ref[0] = dot(grads, acts, TN)


def expert_grads(tokens, grads, acts, gpres):
    parts = len(tokens)
    sources, experts, room, width = tokens[0].shape
    hidden = acts[0].shape[3]
    spec = lambda last: pl.BlockSpec((sources, 1, room, last), lambda e: (0, e, 0, 0))
    out_spec = pl.BlockSpec((1, width, hidden), lambda e: (e, 0, 0))
    out = jax.ShapeDtypeStruct((experts, width, hidden), f32)
    return pl.pallas_call(
        partial(expert_grad_kernel, parts),
        grid=(experts,),
        in_specs=[spec(width)] * (2 * parts) + [spec(hidden)] * (2 * parts),
        out_specs=[out_spec, out_spec],
        out_shape=[out, out],
        compiler_params=PARAMS,
        cost_estimate=cost(4 * parts * sources * experts * room * width * hidden, 8 * experts * width * hidden, 0),
        name="expert_grads",
    )(*tokens, *grads, *acts, *gpres)


def local(
    hidden_in, token_ids, hash_table, deal_order, qkv_weight, out_weight,
    norm1_gain, norm1_bias, norm2_gain, norm2_bias, expert_in, expert_out, out_grad,
):
    devices = lax.axis_size("ctx")
    position = lax.axis_index("ctx")
    planes = lax.axis_size("fsdp")
    plane = lax.axis_index("fsdp")
    width = hidden_in.shape[2]
    local_experts = expert_in.shape[0]
    experts = local_experts * devices
    room = 2 * TOK_DEV // experts
    all_slots = experts * room
    groups = gcd(HEADS, devices)
    cores = devices // groups
    group, core = position // cores, position % cores
    span = width // groups
    across = [[g * cores + c for g in range(groups)] for c in range(cores)]

    own_hidden = hidden_in[0]
    out_cot = out_grad[0]
    evens = range(2, planes, 2)
    packed = (devices, local_experts * room, width)
    shaped = (devices, local_experts, room, width)
    latest = []

    def trade(parts, *args):
        got = plain_trade(after(parts, *latest), *args)
        latest[:] = [got]
        return got

    exchange = lambda rows: trade(rows.reshape(packed), "ctx").reshape(shaped)

    expert_of = hash_table[token_ids[0]]
    same = expert_of[:, None] == expert_of[None, :]
    shape = (TOK_DEV, TOK_DEV)
    before = lax.broadcasted_iota(jnp.int32, shape, 1) < lax.broadcasted_iota(jnp.int32, shape, 0)
    slot = expert_of * room + jnp.sum((same & before).astype(jnp.int32), axis=1)
    counter = lambda axis: lax.broadcasted_iota(
        jnp.int32, (all_slots, TOK_DEV) if axis == 0 else (TOK_DEV, all_slots), axis
    )
    place = lambda s, rows: dot((counter(0) == s[None, :]).astype(bf16), rows).astype(bf16)
    fetch = lambda s, rows: dot(
        (counter(1) == s[:, None]).astype(bf16), rows.reshape(all_slots, width)
    )
    sent = place(slot, out_cot)

    cut = lambda part: lax.dynamic_slice_in_dim(qkv_weight, part * width + group * span, span, 1)
    vecs = jnp.stack([norm1_gain, norm1_bias, norm2_gain, norm2_bias], axis=1)
    lines = width // planes
    codes = jnp.stack([slot // room, slot % room]).astype(bf16).reshape(-1)
    across_lines = -(-codes.shape[0] // lines)
    codes = jnp.pad(codes, (0, across_lines * lines - codes.shape[0])).reshape(lines, across_lines)
    own_cols = jnp.concatenate(
        [cut(0), cut(1), cut(2), vecs, jnp.pad(codes, ((0, 0), (0, 60 - codes.shape[1])))], axis=1
    )
    full = lax.all_gather(own_cols, "fsdp", axis=0, tiled=True)
    wt, vecs = full[:, : 3 * span].T, full[:, 3 * span : 3 * span + 4].T.astype(f32)
    codes = full[:, 3 * span + 4 : 3 * span + 4 + across_lines].reshape(planes, -1)
    codes = codes[:, : 2 * TOK_DEV].astype(jnp.int32)
    all_slot = codes[:, :TOK_DEV] * room + codes[:, TOK_DEV:]
    far_slots = {
        k: lax.dynamic_index_in_dim(all_slot, plane ^ k, 0, False) for k in range(1, planes)
    }
    hidden = [own_hidden] + [swap(own_hidden, "ctx", j * cores) for j in range(1, groups)]
    far_cots = {k: swap(after(out_cot, full), "fsdp", k) for k in evens}

    gys = [None] * planes
    gys[0] = exchange(after(sent, *hidden))
    queries, kvs = zip(project(hidden[:1], wt, vecs), project(hidden[1:], wt, vecs))
    kvs = kvs + tuple(swap(kv, "ctx", k) for k in range(1, cores) for kv in kvs)
    table = deal_order.reshape(groups, cores)
    order = group ^ jnp.arange(groups, dtype=jnp.int32)
    low = jnp.stack(
        [lax.dynamic_index_in_dim(table, core ^ s, 1, False)[order] for s in range(cores)]
    )
    numbers = jnp.stack([low, 2 * devices - 1 - low], axis=2).reshape(-1)
    part = lax.dynamic_index_in_dim(out_weight.reshape(cores, -1, width), core, 0, False)
    part = after(part, full)
    part = [part] + [swap(part, "fsdp", k) for k in range(1, planes)]
    half = list(attend(numbers, order, queries, kvs, None))
    sends = [place(far_slots[k], after(far_cots[k], half[0], *part)) for k in evens]
    half[0] = after(half[0], gys[0], *sends)
    att, att_f, logs = attend(numbers, order, queries, kvs, half)
    part = jnp.stack(in_order(part, plane))
    part = in_order([part] + [swap(part, "ctx", k) for k in range(1, cores)], core)
    out_full = jnp.stack(part, axis=1).reshape(width, width)
    for k, send in zip(evens, sends):
        gys[k] = exchange(send)
    att_t = trade(att, "ctx", across).reshape(width, TOK_DEV)
    gys[1] = swap(after(gys[0], *sends), "fsdp", 1)
    att_t = after(att_t, gys[1])
    middle, normed, sent = middle_step(att_t, own_hidden, out_full, vecs, slot, all_slots)

    tokens, acts, gpres, gns, eys = ([None] * planes for _ in range(5))

    def run(k, *earlier):
        acts[k], gpres[k], gns[k], eys[k] = expert_step(
            after(tokens[k], *earlier), gys[k], expert_in, expert_out
        )

    tokens[0] = exchange(sent)
    run(0)
    done = [acts[0]]
    for k in evens:
        gys[k + 1] = swap(after(gys[k], normed), "fsdp", 1)
        rows = swap(normed, "fsdp", k)
        send = place(far_slots[k], after(rows, *done))
        tokens[k] = exchange(send)
        rows = swap(after(rows, send), "fsdp", 1)
        tokens[k + 1] = exchange(place(far_slots[k + 1], after(rows, gys[k + 1])))
        tokens[1] = swap(after(tokens[0], send), "fsdp", 1)
        run(k)
        run(k + 1, acts[k])
        done = [acts[k + 1]]

    gns[planes - 1] = after(gns[planes - 1], tokens[1])

    far_grad, far_ys = jnp.zeros((TOK_DEV, width), f32), []
    for k in evens:
        last = fetch(far_slots[k + 1], exchange(gns[k + 1])).astype(bf16)
        far_y = swap(eys[k + 1], "fsdp", 1)
        tokens[1] = after(tokens[1], last, far_y)
        far_ys.append((eys[k].astype(f32) + far_y.astype(f32)).astype(bf16))
        back = fetch(far_slots[k], exchange(gns[k]))
        back = (back + swap(last, "fsdp", 1).astype(f32)).astype(bf16)
        far_grad = far_grad + swap(back, "fsdp", k).astype(f32)
    run(1)
    grad_expert_in, grad_expert_out = expert_grads(tokens, gys, acts, gpres)
    near = fetch(far_slots[1], after(exchange(gns[1]), back)).astype(bf16)
    near = swap(near, "fsdp", 1)
    far_grad = (far_grad + near.astype(f32)).astype(bf16)
    got = exchange(gns[0]).reshape(all_slots, width)
    stacked = [p.reshape(packed) for p in [eys[0], eys[1]] + far_ys]
    far_grad = after(far_grad, got, grad_expert_in, *stacked)
    grad_middle, branch, gatt, sums_two = turn_step(
        got, far_grad, slot, middle, out_cot, out_full, vecs
    )
    gatt = trade(gatt.reshape(groups, span, TOK_DEV), "ctx", across)
    outs = out_grad_step(att_t, branch, sums_two, planes, devices)
    stacked = jnp.concatenate(stacked + [outs], axis=1)
    gatt = after(gatt, stacked)
    returned = trade(after(stacked, gatt), "ctx")

    gq, gown, gfar = attend_back(numbers, order, queries, kvs, gatt, att_f, logs)
    got = jnp.stack([swap(gfar[k - 1], "ctx", k) for k in range(1, cores)])
    grad_cols, grad_rows = rows_step(order, gq, gown, got, wt, TOK_DEV)
    came = trade(grad_rows, "ctx", across)
    grad_normed = jnp.sum(came.astype(f32), axis=0)
    mixed = weights_step(order, grad_cols, grad_rows, vecs, hidden, cores, planes)
    own_normal, own_scale = norm_stats(own_hidden.astype(f32))
    grad_hidden = grad_middle + norm_back(own_normal, own_scale, vecs[0], grad_normed)

    def keep(parts, index, axis, stride):
        pick = lambda k: lax.dynamic_index_in_dim(parts, index ^ k, 0, False)
        total = pick(0).astype(f32)
        for k in range(1, parts.shape[0]):
            total = total + swap(pick(k), axis, k * stride).astype(f32)
        return total.astype(bf16)

    size = local_experts * room
    rows = width // planes
    outs = returned[:, (len(evens) + 2) * size :].astype(f32)
    outs = jnp.sum(outs, axis=0).astype(bf16)
    outs, sums = outs[:-16].reshape(planes, rows // devices, width), outs[-16:]
    sums = jnp.broadcast_to(sums[None], (planes,) + sums.shape)
    part = keep(mixed, core, "ctx", 1)
    part = keep(jnp.concatenate([part, outs, sums], axis=1), plane, "fsdp", 1)
    part, sums = part[:-16], part[-16:]
    vec_two = lax.dynamic_slice_in_dim(sums, plane * rows, rows, 1).astype(f32)

    returned = after(returned, part)
    token_y = fetch(slot, returned[:, :size])
    for i, k in enumerate(evens):
        back = fetch(far_slots[k], returned[:, (i + 2) * size : (i + 3) * size]).astype(bf16)
        token_y = token_y + swap(back, "fsdp", k).astype(f32)
    back = fetch(far_slots[1], returned[:, size : 2 * size]).astype(bf16)
    token_y = token_y + swap(back, "fsdp", 1).astype(f32)
    layer_out = (middle + token_y).astype(bf16)

    part = share(part, devices, "ctx", None, trade)
    grad_qkv, vec_one = assemble(part, rows // cores, span, groups)
    part = part[:, rows // cores :].reshape(rows, width).astype(f32)
    return (
        layer_out[None],
        grad_hidden[None],
        grad_qkv,
        part,
        vec_one[:, 0],
        vec_one[:, 1],
        vec_two[0],
        vec_two[1],
        grad_expert_in,
        grad_expert_out,
    )


def solution(mesh):
    return jax.shard_map(
        local,
        mesh=mesh,
        in_specs=(
            P("fsdp", "ctx", None),
            P("fsdp", "ctx"),
            P(),
            P(),
            P("fsdp", None),
            P("fsdp", None),
            P("fsdp"),
            P("fsdp"),
            P("fsdp"),
            P("fsdp"),
            P("ctx", None, "fsdp"),
            P("ctx", None, "fsdp"),
            P("fsdp", "ctx", None),
        ),
        out_specs=(
            P("fsdp", "ctx", None),
            P("fsdp", "ctx", None),
            P("fsdp", None),
            P("fsdp", None),
            P("fsdp"),
            P("fsdp"),
            P("fsdp"),
            P("fsdp"),
            P("ctx", None, "fsdp"),
            P("ctx", None, "fsdp"),
        ),
        check_vma=False,
    )
```

```python
from functools import partial
from math import gcd

import jax
import jax.numpy as jnp
from jax import lax
from jax.experimental import pallas as pl
from jax.experimental.pallas import tpu as pltpu
from jax.sharding import PartitionSpec as P

HEADS = 12
HD = 64
BLK = 256
TOK_DEV = 512
CHUNK = 4
COST = 1000
epsilon = 1e-05
masked_value = -1e30
bf16 = jnp.bfloat16
f32 = jnp.float32
NT = (((1,), (1,)), ((), ()))
NN = (((1,), (0,)), ((), ()))
TN = (((0,), (0,)), ((), ()))
PARAMS = pltpu.CompilerParams(vmem_limit_bytes=56 * 1024 * 1024)


def dot(a, b, dims=NN):
    return lax.dot_general(a, b, dims, preferred_element_type=f32)


def swap(value, axis, offset):
    size = lax.axis_size(axis)
    return lax.ppermute(value, axis, [(i, i ^ offset) for i in range(size)])


def plain_trade(parts, axis, groups=None):
    return lax.all_to_all(parts, axis, 0, 0, tiled=True, axis_index_groups=groups)


def share(part, count, axis, groups, trade):
    return trade(jnp.broadcast_to(part[None], (count,) + part.shape), axis, groups)


def in_order(pieces, index):
    count, bit = len(pieces), 1
    while bit < count:
        odd = (index & bit) != 0
        pieces = [jnp.where(odd, pieces[i ^ bit], pieces[i]) for i in range(count)]
        bit *= 2
    return pieces


def after(value, *others):
    return lax.optimization_barrier((value,) + others)[0]


def norm_stats(values):
    center = jnp.mean(values, axis=-1, keepdims=True)
    offset = values - center
    scale = lax.rsqrt(jnp.mean(offset * offset, axis=-1, keepdims=True) + epsilon)
    return offset * scale, scale


def norm_back(normal, scale, gain, grad):
    inner = grad * gain
    return scale * (
        inner
        - jnp.mean(inner, axis=-1, keepdims=True)
        - normal * jnp.mean(inner * normal, axis=-1, keepdims=True)
    )


def whole(shape):
    return pl.BlockSpec(shape, lambda i, *_: (0,) * len(shape), pipeline_mode=pl.Buffered(1))


def cost(flops, moved, exps=0):
    return pl.CostEstimate(flops=int(flops) // COST, bytes_accessed=int(moved) // COST, transcendentals=int(exps) // COST)


def project_kernel(pieces, *refs):
    wt_ref, vec_ref, q_ref, kv_ref = refs[pieces:]
    span, rows = q_ref.shape[0], refs[0].shape[0]
    for p, ref in enumerate(refs[:pieces]):
        normal, _ = norm_stats(ref[...].astype(f32))
        normed = (normal * vec_ref[0:1] + vec_ref[1:2]).astype(bf16)
        got = dot(wt_ref[...], normed, NT).astype(bf16)
        cut = slice(p * rows, (p + 1) * rows)
        q_ref[:, cut] = (got[:span].astype(f32) * HD ** (-0.5)).astype(bf16)
        kv_ref[:, cut] = got[span:]


def project(hidden, wt, vecs):
    rows, width = hidden[0].shape
    span = wt.shape[0] // 3
    total = len(hidden) * rows
    return pl.pallas_call(
        partial(project_kernel, len(hidden)),
        out_shape=[
            jax.ShapeDtypeStruct((span, total), bf16),
            jax.ShapeDtypeStruct((2 * span, total), bf16),
        ],
        compiler_params=PARAMS,
        cost_estimate=cost(6 * total * width * span, 4 * total * width),
        name="project",
    )(*hidden, wt, vecs)


def only_head(block, head):
    heads = block.shape[0] // HD
    zero = jnp.zeros((HD, block.shape[1]), block.dtype)
    return jnp.concatenate(
        [block[h * HD : (h + 1) * HD] if h == head else zero for h in range(heads)], axis=0
    )


def key_blocks(number_ref, kv_refs, high=1):
    place = 0
    for ref in kv_refs:
        for i in range(ref.shape[1] // BLK):
            if high or i % 2 == 0:
                at = pl.multiple_of(number_ref[place] * BLK, BLK)
                yield at, ref[:, i * BLK : (i + 1) * BLK]
            place += 1


def take_queries(q_refs, q_all):
    at = 0
    for ref in q_refs:
        q_all[:, at : at + ref.shape[1]] = ref[...]
        at += ref.shape[1]


def attend_kernel(high, parts, all_parts, number_ref, order_ref, *refs):
    q_refs, kv_refs = refs[:parts], refs[parts:all_parts]
    att_ref, att_t_ref, lse_ref, acc_ref, q_all, k_sorted, v_sorted = refs[-7:]
    turn = pl.program_id(0)
    span = acc_ref.shape[0]
    heads = span // HD
    block = number_ref[2 * turn + high]
    size = CHUNK * BLK

    @pl.when(turn == 0)
    def _():
        take_queries(q_refs, q_all)
        for at, kv in key_blocks(number_ref, kv_refs, high):
            k_sorted[pl.ds(at, BLK), :] = jnp.transpose(kv[:span])
            v_sorted[:, pl.ds(at, BLK)] = kv[span:]

    own_queries = q_all[:, pl.ds(pl.multiple_of((2 * turn + high) * BLK, BLK), BLK)]
    queries = [only_head(own_queries, h) for h in range(heads)]
    acc_ref[...] = jnp.zeros_like(acc_ref)

    def step(last, index, state):
        top, total = state
        at = pl.multiple_of(index * size, size)
        keys = k_sorted[pl.ds(at, size), :]
        tops, totals = [], []
        scores = [dot(keys, queries[h]) for h in range(heads)]
        if last:
            row = lax.broadcasted_iota(jnp.int32, scores[0].shape, 0)
            limit = (block + 1 - index * CHUNK) * BLK
            scores = [jnp.where(row < limit, s, masked_value) for s in scores]
        for h in range(heads):
            rows = slice(h * HD, (h + 1) * HD)
            new_top = jnp.maximum(top[h], jnp.max(scores[h], axis=0, keepdims=True))
            factor = jnp.exp(top[h] - new_top)
            weights = jnp.exp(scores[h] - new_top)
            tops.append(new_top)
            totals.append(total[h] * factor + jnp.sum(weights, axis=0, keepdims=True))
            update = dot(v_sorted[rows, pl.ds(at, size)], weights.astype(bf16))
            acc_ref[rows, :] = acc_ref[rows, :] * factor + update
        return tuple(tops), tuple(totals)

    start = (
        tuple(jnp.full((1, BLK), masked_value, f32) for _ in range(heads)),
        tuple(jnp.zeros((1, BLK), f32) for _ in range(heads)),
    )
    full = (block + 1) // CHUNK
    state = lax.fori_loop(0, full, partial(step, False), start)
    top, total = lax.fori_loop(full, (block + CHUNK) // CHUNK, partial(step, True), state)
    for h in range(heads):
        rows = slice(h * HD, (h + 1) * HD)
        out = acc_ref[rows, :] / total[h]
        att_t_ref[rows, :] = out
        att_ref[0, rows, :] = out.astype(bf16)
        lse_ref[0, h : h + 1, :] = top[h] + jnp.log(total[h])


def attend(numbers, order, queries, kvs, before):
    high = 0 if before is None else 1
    before = () if before is None else tuple(before)
    pieces, span = order.shape[0], queries[0].shape[0]
    rows, keys = sum(q.shape[1] for q in queries), sum(kv.shape[1] for kv in kvs)
    piece, blocks = rows // pieces, rows // BLK
    sorted_keys = keys if high else keys // 2
    return pl.pallas_call(
        partial(attend_kernel, high, len(queries), len(queries + kvs)),
        grid_spec=pltpu.PrefetchScalarGridSpec(
            num_scalar_prefetch=2,
            grid=(blocks // 2,),
            in_specs=[whole(a.shape) for a in queries + kvs]
            + [pl.BlockSpec(memory_space=pl.ANY)] * len(before),
            out_specs=[
                pl.BlockSpec((1, span, BLK), lambda i, n, o: (o[i], 0, high)),
                pl.BlockSpec((span, BLK), lambda i, *_: (0, 2 * i + high)),
                pl.BlockSpec((1, 8, BLK), lambda i, *_: (2 * i + high, 0, 0)),
            ],
            scratch_shapes=[
                pltpu.VMEM((span, BLK), f32),
                pltpu.VMEM((span, rows), bf16),
                pltpu.VMEM((sorted_keys, span), bf16),
                pltpu.VMEM((span, sorted_keys), bf16),
            ],
        ),
        out_shape=[
            jax.ShapeDtypeStruct((pieces, span, piece), bf16),
            jax.ShapeDtypeStruct((span, rows), f32),
            jax.ShapeDtypeStruct((blocks, 8, BLK), f32),
        ],
        compiler_params=PARAMS,
        cost_estimate=cost(12 * rows * keys * span, 8 * keys * span, rows * keys * span // 128),
        input_output_aliases={2 + len(queries + kvs) + i: i for i in range(len(before))},
        name="attend_high" if high else "attend_low",
    )(numbers, order, *queries, *kvs, *before)


def attend_back_kernel(parts, all_parts, number_ref, order_ref, g_ref, att_t_ref, lse_ref, *refs):
    q_refs, kv_refs = refs[:parts], refs[parts:all_parts]
    gq_ref, gown_ref, gfar_ref = refs[all_parts : all_parts + 3]
    gq_acc, gk_acc, gv_acc, q_all, k_sorted, v_sorted, kt_sorted = refs[all_parts + 3 :]
    sides = 1 + gfar_ref.shape[0]
    turn = pl.program_id(0)
    span = gq_acc.shape[0]
    heads = span // HD
    block = number_ref[turn]
    size = CHUNK * BLK

    @pl.when(turn == 0)
    def _():
        gk_acc[...] = jnp.zeros_like(gk_acc)
        gv_acc[...] = jnp.zeros_like(gv_acc)
        take_queries(q_refs, q_all)
        for at, kv in key_blocks(number_ref, kv_refs):
            k_sorted[pl.ds(at, BLK), :] = jnp.transpose(kv[:span])
            v_sorted[pl.ds(at, BLK), :] = jnp.transpose(kv[span:])
            kt_sorted[:, pl.ds(at, BLK)] = kv[:span]

    grads = g_ref[0]
    queries = q_all[:, pl.ds(pl.multiple_of(turn * BLK, BLK), BLK)]
    prod = grads.astype(f32) * att_t_ref[...]
    part = lambda h: slice(h * HD, (h + 1) * HD)
    deltas = [jnp.sum(prod[part(h)], axis=0, keepdims=True) for h in range(heads)]
    logs = [lse_ref[0, h : h + 1, :] for h in range(heads)]
    q_only = [only_head(queries, h) for h in range(heads)]
    g_only = [only_head(grads, h) for h in range(heads)]
    gq_acc[...] = jnp.zeros_like(gq_acc)

    def step(last, index, carry):
        at = pl.multiple_of(index * size, size)
        keys = k_sorted[pl.ds(at, size), :]
        values = v_sorted[pl.ds(at, size), :]
        if last:
            row = lax.broadcasted_iota(jnp.int32, (size, BLK), 0)
            allowed = row < (block + 1 - index * CHUNK) * BLK
        for h in range(heads):
            rows = part(h)
            probs = jnp.exp(dot(keys, q_only[h]) - logs[h])
            if last:
                probs = jnp.where(allowed, probs, 0.0)
            gs = (probs * (dot(values, g_only[h]) - deltas[h])).astype(bf16)
            gq_acc[rows, :] += dot(kt_sorted[rows, pl.ds(at, size)], gs)
            gv_acc[rows, pl.ds(at, size)] += dot(grads[rows], probs.astype(bf16), NT)
            gk_acc[rows, pl.ds(at, size)] += dot(queries[rows], gs, NT)
        return carry

    full = (block + 1) // CHUNK
    lax.fori_loop(0, full, partial(step, False), 0)
    lax.fori_loop(full, (block + CHUNK) // CHUNK, partial(step, True), 0)
    gq_ref[...] = (gq_acc[...] * HD ** (-0.5)).astype(bf16)

    @pl.when(turn == pl.num_programs(0) - 1)
    def _():
        per = gown_ref.shape[1] // BLK
        for s in range(sides):
            for i in range(per):
                at = pl.multiple_of(number_ref[s * per + i] * BLK, BLK)
                cut = slice(i * BLK, (i + 1) * BLK)
                gk = gk_acc[:, pl.ds(at, BLK)].astype(bf16)
                gv = gv_acc[:, pl.ds(at, BLK)].astype(bf16)
                if s == 0:
                    gown_ref[:span, cut], gown_ref[span:, cut] = gk, gv
                else:
                    gfar_ref[s - 1, :span, cut], gfar_ref[s - 1, span:, cut] = gk, gv


def attend_back(numbers, order, queries, kvs, grads, att_t, logs):
    span = queries[0].shape[0]
    rows, keys = sum(q.shape[1] for q in queries), sum(kv.shape[1] for kv in kvs)
    sides, blocks = keys // rows, rows // BLK
    column = pl.BlockSpec((span, BLK), lambda i, *_: (0, i))
    return pl.pallas_call(
        partial(attend_back_kernel, len(queries), len(queries + kvs)),
        grid_spec=pltpu.PrefetchScalarGridSpec(
            num_scalar_prefetch=2,
            grid=(blocks,),
            in_specs=[
                pl.BlockSpec((1, span, BLK), lambda i, n, o: (o[i // 2], 0, i % 2)),
                column,
                pl.BlockSpec((1, 8, BLK), lambda i, *_: (i, 0, 0)),
            ]
            + [whole(a.shape) for a in queries + kvs],
            out_specs=[column, whole((2 * span, rows)), whole((sides - 1, 2 * span, rows))],
            scratch_shapes=[
                pltpu.VMEM((span, BLK), f32),
                pltpu.VMEM((span, keys), f32),
                pltpu.VMEM((span, keys), f32),
                pltpu.VMEM((span, rows), bf16),
                pltpu.VMEM((keys, span), bf16),
                pltpu.VMEM((keys, span), bf16),
                pltpu.VMEM((span, keys), bf16),
            ],
        ),
        out_shape=[
            jax.ShapeDtypeStruct((span, rows), bf16),
            jax.ShapeDtypeStruct((2 * span, rows), bf16),
            jax.ShapeDtypeStruct((sides - 1, 2 * span, rows), bf16),
        ],
        compiler_params=PARAMS,
        cost_estimate=cost(30 * rows * keys * span, 16 * keys * span, rows * keys * span // 128),
        name="attend_back",
    )(numbers, order, grads, att_t, logs, *queries, *kvs)


def middle_kernel(att_ref, x_ref, w_ref, vec_ref, slot_ref, mid_ref, normed_ref, send_ref):
    middle = x_ref[...].astype(f32) + dot(att_ref[...], w_ref[...], TN)
    normal, _ = norm_stats(middle)
    normed = (normal * vec_ref[2:3] + vec_ref[3:4]).astype(bf16)
    mid_ref[...] = middle
    normed_ref[...] = normed
    slots = lax.broadcasted_iota(jnp.int32, (send_ref.shape[0], x_ref.shape[0]), 0)
    place = (slots == slot_ref[...]).astype(f32).astype(bf16)
    send_ref[...] = dot(place, normed).astype(bf16)


def middle_step(att_t, rows, weight, vecs, slot, all_slots):
    count, width = rows.shape
    return pl.pallas_call(
        middle_kernel,
        out_shape=[
            jax.ShapeDtypeStruct((count, width), f32),
            jax.ShapeDtypeStruct((count, width), bf16),
            jax.ShapeDtypeStruct((all_slots, width), bf16),
        ],
        compiler_params=PARAMS,
        cost_estimate=cost(2 * count * width * (width + all_slots), 10 * count * width),
        name="middle",
    )(att_t, rows, weight, vecs, slot[None, :])


def turn_kernel(
    got_ref, far_ref, slot_ref, mid_ref, cot_ref, w_ref, vec_ref, gmid_ref, gbr_ref, gatt_ref, sum_ref
):
    slots = lax.broadcasted_iota(jnp.int32, (mid_ref.shape[0], got_ref.shape[0]), 1)
    place = (slots == slot_ref[...]).astype(f32).astype(bf16)
    grad = (dot(place, got_ref[...]) + far_ref[...].astype(f32)).astype(bf16).astype(f32)
    normal, scale = norm_stats(mid_ref[...])
    middle = cot_ref[...].astype(f32) + norm_back(normal, scale, vec_ref[2:3], grad)
    branch = middle.astype(bf16)
    gmid_ref[...] = middle
    gbr_ref[...] = branch
    gatt_ref[...] = dot(w_ref[...], branch, NT).astype(bf16)
    sum_ref[...] = jnp.zeros_like(sum_ref)
    sum_ref[0:1] = jnp.sum(grad * normal, axis=0, keepdims=True)
    sum_ref[1:2] = jnp.sum(grad, axis=0, keepdims=True)


def turn_step(got, far, slot, middle, cot, weight, vecs):
    count, width = middle.shape
    return pl.pallas_call(
        turn_kernel,
        out_shape=[
            jax.ShapeDtypeStruct((count, width), f32),
            jax.ShapeDtypeStruct((count, width), bf16),
            jax.ShapeDtypeStruct((weight.shape[0], count), bf16),
            jax.ShapeDtypeStruct((128, width), f32),
        ],
        compiler_params=PARAMS,
        cost_estimate=cost(2 * count * width * (width + got.shape[0]), 12 * count * width),
        name="turn",
    )(got, far, slot[:, None], middle, cot, weight, vecs)


def out_grad_kernel(planes, att_ref, gbr_ref, sum_ref, out_ref):
    count = out_ref.shape[0]
    weights = dot(att_ref[...], gbr_ref[...])
    step = weights.shape[0] // (planes * count)
    for c in range(count):
        at = [(z * count + c) * step for z in range(planes)]
        pieces = [weights[a : a + step] for a in at] + [sum_ref[:16]]
        out_ref[c] = jnp.concatenate(pieces, axis=0).astype(bf16)


def out_grad_step(att_t, gbr, sums, planes, devices):
    rows = att_t.shape[0] // devices + 16
    return pl.pallas_call(
        partial(out_grad_kernel, planes),
        out_shape=jax.ShapeDtypeStruct((devices, rows, gbr.shape[1]), bf16),
        compiler_params=PARAMS,
        cost_estimate=cost(2 * att_t.size * gbr.shape[1], 6 * gbr.size),
        name="out_grad",
    )(att_t, gbr, sums)


def rows_kernel(order_ref, gq_ref, gown_ref, got_ref, wt_ref, cols_ref, out_ref):
    rows = out_ref.shape[1]
    for j in range(out_ref.shape[0]):
        cut = slice(j * rows, (j + 1) * rows)
        gkv = gown_ref[:, cut].astype(f32)
        for k in range(got_ref.shape[0]):
            gkv = gkv + got_ref[k, :, cut].astype(f32)
        columns = jnp.concatenate([gq_ref[:, cut], gkv.astype(bf16)], axis=0)
        cols_ref[:, cut] = columns
        out_ref[order_ref[j]] = dot(columns, wt_ref[...], TN).astype(bf16)


SCALARS = pl.BlockSpec(memory_space=pltpu.SMEM)
ARRAY = pl.BlockSpec(memory_space=pltpu.VMEM)


def rows_step(order, gq, gown, got, wt, rows):
    sources = gq.shape[1] // rows
    wide, width = wt.shape
    return pl.pallas_call(
        rows_kernel,
        in_specs=[SCALARS] + [ARRAY] * 4,
        out_shape=[
            jax.ShapeDtypeStruct((wide, sources * rows), bf16),
            jax.ShapeDtypeStruct((sources, rows, width), bf16),
        ],
        compiler_params=PARAMS,
        cost_estimate=cost(2 * sources * rows * width * wide, 4 * sources * rows * width),
        name="rows",
    )(order, gq, gown, got, wt)


def weights_kernel(order_ref, cols_ref, vec_ref, rows_ref, *refs):
    hidden_refs, mixed_ref = refs[:-1], refs[-1]
    piece = rows_ref.shape[1]
    total, gains, biases = None, 0.0, 0.0
    for j, ref in enumerate(hidden_refs):
        normal, _ = norm_stats(ref[...].astype(f32))
        normed = (normal * vec_ref[0:1] + vec_ref[1:2]).astype(bf16)
        rows = rows_ref[order_ref[j]].astype(f32)
        gains += jnp.sum(rows * normal, axis=0, keepdims=True)
        biases += jnp.sum(rows, axis=0, keepdims=True)
        part = dot(cols_ref[:, j * piece : (j + 1) * piece], normed)
        total = part if total is None else total + part
    cores, planes, count, _ = mixed_ref.shape
    wide = total.shape[0]
    weights = jnp.transpose(total).astype(bf16)
    zeros = jnp.zeros((126, total.shape[1]), f32)
    sums = jnp.transpose(jnp.concatenate([gains, biases, zeros], axis=0)).astype(bf16)
    for z in range(planes):
        for s in range(cores):
            at = (z * cores + s) * count
            mixed_ref[s, z, :, :wide] = weights[at : at + count]
            mixed_ref[s, z, :, wide : wide + 128] = sums[at : at + count]
            rest = mixed_ref.shape[3] - wide - 128
            mixed_ref[s, z, :, wide + 128 :] = jnp.zeros((count, rest), bf16)


def weights_step(order, cols, rows, vecs, hidden, cores, planes):
    wide, width = cols.shape[0], rows.shape[2]
    shape = (cores, planes, width // (cores * planes), width)
    return pl.pallas_call(
        weights_kernel,
        in_specs=[SCALARS] + [ARRAY] * (3 + len(hidden)),
        out_shape=jax.ShapeDtypeStruct(shape, bf16),
        compiler_params=PARAMS,
        cost_estimate=cost(2 * cols.size * width, 4 * cols.size),
        name="weights",
    )(order, cols, vecs, rows, *hidden)


def assemble_kernel(span, groups, part_ref, out_ref, sum_ref):
    count, rows = part_ref.shape[0], out_ref.shape[0] // (part_ref.shape[0] // groups)
    cores = count // groups
    for s in range(cores):
        at = slice(s * rows, (s + 1) * rows)
        pieces = [part_ref[g * cores + s, :rows].astype(f32) for g in range(groups)]
        out_ref[at, :] = jnp.concatenate(
            [p[:, t * span : (t + 1) * span] for t in range(3) for p in pieces], axis=1
        )
        sum_ref[at, :] = sum(p[:, 3 * span : 3 * span + 128] for p in pieces)


def assemble(part, rows, span, groups):
    count = part.shape[0]
    total = rows * (count // groups)
    return pl.pallas_call(
        partial(assemble_kernel, span, groups),
        out_shape=[
            jax.ShapeDtypeStruct((total, 3 * span * groups), f32),
            jax.ShapeDtypeStruct((total, 128), f32),
        ],
        compiler_params=PARAMS,
        cost_estimate=cost(part.size, 6 * part.size),
        name="assemble",
    )(part)


def expert_kernel(x_ref, gy_ref, first_ref, second_ref, act_ref, gpre_ref, gn_ref, ey_ref):
    flat = lambda ref: ref[...].reshape(-1, ref.shape[-1])
    first, second = first_ref[0], second_ref[0]
    pre = dot(flat(x_ref), first)
    inner = 0.7978845608028654 * (pre + 0.044715 * (pre * pre * pre))
    bend = jnp.tanh(inner)
    half = 0.5 * (1.0 + bend)
    act = (pre * half).astype(bf16)
    slope = half + 0.5 * pre * (1.0 - bend * bend) * (
        0.7978845608028654 * (1.0 + 3 * 0.044715 * (pre * pre))
    )
    gpre = (dot(flat(gy_ref), second) * slope).astype(bf16)
    act_ref[...] = act.reshape(act_ref.shape)
    gpre_ref[...] = gpre.reshape(gpre_ref.shape)
    gn_ref[...] = dot(gpre, first, NT).astype(bf16).reshape(gn_ref.shape)
    ey_ref[...] = dot(act, second, NT).astype(bf16).reshape(ey_ref.shape)


def expert_step(tokens, grads, first, second):
    sources, experts, room, width = tokens.shape
    hidden = first.shape[2]
    token_spec = pl.BlockSpec((sources, 1, room, width), lambda e: (0, e, 0, 0))
    hidden_spec = pl.BlockSpec((sources, 1, room, hidden), lambda e: (0, e, 0, 0))
    weight_spec = pl.BlockSpec((1, width, hidden), lambda e: (e, 0, 0))
    like = lambda last: jax.ShapeDtypeStruct((sources, experts, room, last), bf16)
    return pl.pallas_call(
        expert_kernel,
        grid=(experts,),
        in_specs=[token_spec, token_spec, weight_spec, weight_spec],
        out_specs=[hidden_spec, hidden_spec, token_spec, token_spec],
        out_shape=[like(hidden), like(hidden), like(width), like(width)],
        compiler_params=PARAMS,
        cost_estimate=cost(8 * sources * experts * room * width * hidden, 4 * first.size + 12 * tokens.size, sources * experts * room * hidden),
        name="expert_step",
    )(tokens, grads, first, second)


def expert_grad_kernel(parts, *refs):
    flat = lambda ref: ref[...].reshape(-1, ref.shape[-1])
    stack = lambda some: jnp.concatenate([flat(r) for r in some], axis=0)
    ins, (gfirst_ref, gsecond_ref) = refs[: 4 * parts], refs[4 * parts :]
    tokens, grads, acts, gpres = (stack(ins[i * parts : (i + 1) * parts]) for i in range(4))
    gfirst_ref[0] = dot(tokens, gpres, TN)
    gsecond_ref[0] = dot(grads, acts, TN)


def expert_grads(tokens, grads, acts, gpres):
    parts = len(tokens)
    sources, experts, room, width = tokens[0].shape
    hidden = acts[0].shape[3]
    spec = lambda last: pl.BlockSpec((sources, 1, room, last), lambda e: (0, e, 0, 0))
    out_spec = pl.BlockSpec((1, width, hidden), lambda e: (e, 0, 0))
    out = jax.ShapeDtypeStruct((experts, width, hidden), f32)
    return pl.pallas_call(
        partial(expert_grad_kernel, parts),
        grid=(experts,),
        in_specs=[spec(width)] * (2 * parts) + [spec(hidden)] * (2 * parts),
        out_specs=[out_spec, out_spec],
        out_shape=[out, out],
        compiler_params=PARAMS,
        cost_estimate=cost(4 * parts * sources * experts * room * width * hidden, 8 * experts * width * hidden, 0),
        name="expert_grads",
    )(*tokens, *grads, *acts, *gpres)


def local(
    hidden_in, token_ids, hash_table, deal_order, qkv_weight, out_weight,
    norm1_gain, norm1_bias, norm2_gain, norm2_bias, expert_in, expert_out, out_grad,
):
    devices = lax.axis_size("ctx")
    position = lax.axis_index("ctx")
    planes = lax.axis_size("fsdp")
    plane = lax.axis_index("fsdp")
    width = hidden_in.shape[2]
    local_experts = expert_in.shape[0]
    experts = local_experts * devices
    room = 2 * TOK_DEV // experts
    all_slots = experts * room
    groups = gcd(HEADS, devices)
    cores = devices // groups
    group, core = position // cores, position % cores
    span = width // groups
    across = [[g * cores + c for g in range(groups)] for c in range(cores)]

    own_hidden = hidden_in[0]
    out_cot = out_grad[0]
    evens = range(2, planes, 2)
    packed = (devices, local_experts * room, width)
    shaped = (devices, local_experts, room, width)
    latest = []

    def trade(parts, *args):
        got = plain_trade(after(parts, *latest), *args)
        latest[:] = [got]
        return got

    exchange = lambda rows: trade(rows.reshape(packed), "ctx").reshape(shaped)

    expert_of = hash_table[token_ids[0]]
    same = expert_of[:, None] == expert_of[None, :]
    shape = (TOK_DEV, TOK_DEV)
    before = lax.broadcasted_iota(jnp.int32, shape, 1) < lax.broadcasted_iota(jnp.int32, shape, 0)
    slot = expert_of * room + jnp.sum((same & before).astype(jnp.int32), axis=1)
    counter = lambda axis: lax.broadcasted_iota(
        jnp.int32, (all_slots, TOK_DEV) if axis == 0 else (TOK_DEV, all_slots), axis
    )
    place = lambda s, rows: dot((counter(0) == s[None, :]).astype(bf16), rows).astype(bf16)
    fetch = lambda s, rows: dot(
        (counter(1) == s[:, None]).astype(bf16), rows.reshape(all_slots, width)
    )
    sent = place(slot, out_cot)

    cut = lambda part: lax.dynamic_slice_in_dim(qkv_weight, part * width + group * span, span, 1)
    vecs = jnp.stack([norm1_gain, norm1_bias, norm2_gain, norm2_bias], axis=1)
    lines = width // planes
    codes = jnp.stack([slot // room, slot % room]).astype(bf16).reshape(-1)
    across_lines = -(-codes.shape[0] // lines)
    codes = jnp.pad(codes, (0, across_lines * lines - codes.shape[0])).reshape(lines, across_lines)
    own_cols = jnp.concatenate(
        [cut(0), cut(1), cut(2), vecs, jnp.pad(codes, ((0, 0), (0, 60 - codes.shape[1])))], axis=1
    )
    full = lax.all_gather(own_cols, "fsdp", axis=0, tiled=True)
    wt, vecs = full[:, : 3 * span].T, full[:, 3 * span : 3 * span + 4].T.astype(f32)
    codes = full[:, 3 * span + 4 : 3 * span + 4 + across_lines].reshape(planes, -1)
    codes = codes[:, : 2 * TOK_DEV].astype(jnp.int32)
    all_slot = codes[:, :TOK_DEV] * room + codes[:, TOK_DEV:]
    far_slots = {
        k: lax.dynamic_index_in_dim(all_slot, plane ^ k, 0, False) for k in range(1, planes)
    }
    hidden = [own_hidden] + [swap(own_hidden, "ctx", j * cores) for j in range(1, groups)]
    far_cots = {k: swap(after(out_cot, full), "fsdp", k) for k in evens}

    gys = [None] * planes
    gys[0] = exchange(after(sent, *hidden))
    queries, kvs = zip(project(hidden[:1], wt, vecs), project(hidden[1:], wt, vecs))
    kvs = kvs + tuple(swap(kv, "ctx", k) for k in range(1, cores) for kv in kvs)
    table = deal_order.reshape(groups, cores)
    order = group ^ jnp.arange(groups, dtype=jnp.int32)
    low = jnp.stack(
        [lax.dynamic_index_in_dim(table, core ^ s, 1, False)[order] for s in range(cores)]
    )
    numbers = jnp.stack([low, 2 * devices - 1 - low], axis=2).reshape(-1)
    part = lax.dynamic_index_in_dim(out_weight.reshape(cores, -1, width), core, 0, False)
    part = after(part, full)
    part = [part] + [swap(part, "fsdp", k) for k in range(1, planes)]
    half = list(attend(numbers, order, queries, kvs, None))
    sends = [place(far_slots[k], after(far_cots[k], half[0], *part)) for k in evens]
    half[0] = after(half[0], gys[0], *sends)
    att, att_f, logs = attend(numbers, order, queries, kvs, half)
    part = jnp.stack(in_order(part, plane))
    part = in_order([part] + [swap(part, "ctx", k) for k in range(1, cores)], core)
    out_full = jnp.stack(part, axis=1).reshape(width, width)
    for k, send in zip(evens, sends):
        gys[k] = exchange(send)
    att_t = trade(att, "ctx", across).reshape(width, TOK_DEV)
    gys[1] = swap(after(gys[0], *sends), "fsdp", 1)
    att_t = after(att_t, gys[1])
    middle, normed, sent = middle_step(att_t, own_hidden, out_full, vecs, slot, all_slots)

    tokens, acts, gpres, gns, eys = ([None] * planes for _ in range(5))

    def run(k, *earlier):
        acts[k], gpres[k], gns[k], eys[k] = expert_step(
            after(tokens[k], *earlier), gys[k], expert_in, expert_out
        )

    tokens[0] = exchange(sent)
    run(0)
    done = [acts[0]]
    for k in evens:
        gys[k + 1] = swap(after(gys[k], normed), "fsdp", 1)
        rows = swap(normed, "fsdp", k)
        send = place(far_slots[k], after(rows, *done))
        tokens[k] = exchange(send)
        rows = swap(after(rows, send), "fsdp", 1)
        tokens[k + 1] = exchange(place(far_slots[k + 1], after(rows, gys[k + 1])))
        tokens[1] = swap(after(tokens[0], send), "fsdp", 1)
        run(k)
        run(k + 1, acts[k])
        done = [acts[k + 1]]

    gns[planes - 1] = after(gns[planes - 1], tokens[1])

    far_grad, far_ys = jnp.zeros((TOK_DEV, width), f32), []
    for k in evens:
        last = fetch(far_slots[k + 1], exchange(gns[k + 1])).astype(bf16)
        far_y = swap(eys[k + 1], "fsdp", 1)
        tokens[1] = after(tokens[1], last, far_y)
        far_ys.append((eys[k].astype(f32) + far_y.astype(f32)).astype(bf16))
        back = fetch(far_slots[k], exchange(gns[k]))
        back = (back + swap(last, "fsdp", 1).astype(f32)).astype(bf16)
        far_grad = far_grad + swap(back, "fsdp", k).astype(f32)
    run(1)
    grad_expert_in, grad_expert_out = expert_grads(tokens, gys, acts, gpres)
    near = fetch(far_slots[1], after(exchange(gns[1]), back)).astype(bf16)
    near = swap(near, "fsdp", 1)
    far_grad = (far_grad + near.astype(f32)).astype(bf16)
    got = exchange(gns[0]).reshape(all_slots, width)
    stacked = [p.reshape(packed) for p in [eys[0], eys[1]] + far_ys]
    far_grad = after(far_grad, got, grad_expert_in, *stacked)
    grad_middle, branch, gatt, sums_two = turn_step(
        got, far_grad, slot, middle, out_cot, out_full, vecs
    )
    gatt = trade(gatt.reshape(groups, span, TOK_DEV), "ctx", across)
    outs = out_grad_step(att_t, branch, sums_two, planes, devices)
    stacked = jnp.concatenate(stacked + [outs], axis=1)
    gatt = after(gatt, stacked)
    returned = trade(after(stacked, gatt), "ctx")

    gq, gown, gfar = attend_back(numbers, order, queries, kvs, gatt, att_f, logs)
    got = jnp.stack([swap(gfar[k - 1], "ctx", k) for k in range(1, cores)])
    grad_cols, grad_rows = rows_step(order, gq, gown, got, wt, TOK_DEV)
    came = trade(grad_rows, "ctx", across)
    grad_normed = jnp.sum(came.astype(f32), axis=0)
    mixed = weights_step(order, grad_cols, grad_rows, vecs, hidden, cores, planes)
    own_normal, own_scale = norm_stats(own_hidden.astype(f32))
    grad_hidden = grad_middle + norm_back(own_normal, own_scale, vecs[0], grad_normed)

    def keep(parts, index, axis, stride):
        pick = lambda k: lax.dynamic_index_in_dim(parts, index ^ k, 0, False)
        total = pick(0).astype(f32)
        for k in range(1, parts.shape[0]):
            total = total + swap(pick(k), axis, k * stride).astype(f32)
        return total.astype(bf16)

    size = local_experts * room
    rows = width // planes
    outs = returned[:, (len(evens) + 2) * size :].astype(f32)
    outs = jnp.sum(outs, axis=0).astype(bf16)
    outs, sums = outs[:-16].reshape(planes, rows // devices, width), outs[-16:]
    sums = jnp.broadcast_to(sums[None], (planes,) + sums.shape)
    part = keep(mixed, core, "ctx", 1)
    part = keep(jnp.concatenate([part, outs, sums], axis=1), plane, "fsdp", 1)
    part, sums = part[:-16], part[-16:]
    vec_two = lax.dynamic_slice_in_dim(sums, plane * rows, rows, 1).astype(f32)

    returned = after(returned, part)
    token_y = fetch(slot, returned[:, :size])
    for i, k in enumerate(evens):
        back = fetch(far_slots[k], returned[:, (i + 2) * size : (i + 3) * size]).astype(bf16)
        token_y = token_y + after(swap(back, "fsdp", k), grad_hidden).astype(f32)
    back = fetch(far_slots[1], returned[:, size : 2 * size]).astype(bf16)
    token_y = token_y + after(swap(back, "fsdp", 1), grad_hidden).astype(f32)
    layer_out = (middle + token_y).astype(bf16)

    part = share(part, devices, "ctx", None, trade)
    grad_qkv, vec_one = assemble(part, rows // cores, span, groups)
    part = part[:, rows // cores :].reshape(rows, width).astype(f32)
    return (
        layer_out[None],
        grad_hidden[None],
        grad_qkv,
        part,
        vec_one[:, 0],
        vec_one[:, 1],
        vec_two[0],
        vec_two[1],
        grad_expert_in,
        grad_expert_out,
    )


def solution(mesh):
    return jax.shard_map(
        local,
        mesh=mesh,
        in_specs=(
            P("fsdp", "ctx", None),
            P("fsdp", "ctx"),
            P(),
            P(),
            P("fsdp", None),
            P("fsdp", None),
            P("fsdp"),
            P("fsdp"),
            P("fsdp"),
            P("fsdp"),
            P("ctx", None, "fsdp"),
            P("ctx", None, "fsdp"),
            P("fsdp", "ctx", None),
        ),
        out_specs=(
            P("fsdp", "ctx", None),
            P("fsdp", "ctx", None),
            P("fsdp", None),
            P("fsdp", None),
            P("fsdp"),
            P("fsdp"),
            P("fsdp"),
            P("fsdp"),
            P("ctx", None, "fsdp"),
            P("ctx", None, "fsdp"),
        ),
        check_vma=False,
    )
```
